256 devices in a mesh: dp: 8 (over y, x_lo), context: 8 (over z), tensor: 4 (over x_hi, core).
Axes of the slice: x: 4 (x_hi: 2, x_lo: 2; x = x_hi * 2 + x_lo), y: 4, z: 8, core: 2. Of those that a mesh axis runs over, the one named last changes fastest.
Arguments:
- layer_input: bfloat16 [8, 4096, 8192], P('dp', 'context'), may hold values from -60 to 60
- queries: bfloat16 [8, 4096, 4096], P('dp', 'context', 'tensor'), may hold values from -6 to 6
- rotated_key_states: bfloat16 [8, 4096, 512], P('dp', 'context', 'tensor'), may hold values from -6 to 6
- values: bfloat16 [8, 4096, 512], P('dp', 'context', 'tensor'), may hold values from -6 to 6
- attention_out: bfloat16 [8, 4096, 4096], P('dp', 'context', 'tensor'), may hold values from -6 to 6
- output_grad: bfloat16 [8, 4096, 4096], P('dp', 'context', 'tensor'), may hold values from -6 to 6
- normalizer_shift: float32 [32], P('tensor'), may hold values from 0 to 1.5
- document_lengths: int32 [8, 16], P('dp'), may hold values from 1 to 3072, 4096 in all within a row
- dither: int32 [2, 8192, 512], P(None, ('dp', 'context'), 'tensor'), may hold values from 0 to 255
Outputs:
- query_grad: bfloat16 [8, 4096, 4096], P('dp', 'context', 'tensor')
- weight_codes: float32 [2, 8192, 512], P(None, ('dp', 'context'), 'tensor')
The draws below stay inside these ranges and needn't reach their ends.
Inputs may be any that keep to these rules, and one draw needn't show every extreme that they name: `document_lengths`: each sequence's lengths sum to 4096, and its longest document has exactly 3072 positions.
All inputs are finite; a program needn't handle non-finite values. Where the reference program divides by a largest or mean magnitude, that divisor is 1e-20 or more.
Results may differ from the reference program's by a relative error of at most 0.0064.
Values may be sent and summed in bfloat16 or wider, within the bound.
No kernel may reach another device: no remote copies, remote signals or barrier semaphores. Data moves between devices by JAX's collectives and lax.ppermute only.
A program may use at most 64 MiB of HBM per device.

```python
import math
import jax
import jax.numpy as jnp
import numpy as np
from jax import lax

MODEL_WIDTH = 8192
QUERY_HEADS = 32
KEY_VALUE_HEADS = 4
HEAD_SIZE = 128
NDOC = 16
CODE_BLOCK_ROWS = 128
BATCH_SEQUENCES = 8
SEQUENCE_LENGTH = 4096


def draw_layer_input(key, part):
    key = jax.random.fold_in(key, 11)
    first, second, third = jax.random.split(key, 3)
    row_scale = jnp.exp(jax.random.uniform(second, (BATCH_SEQUENCES, SEQUENCE_LENGTH, 1), jnp.float32, 0.0, math.log(10.0)))
    column_scale = jnp.exp(jax.random.uniform(third, (1, 1, MODEL_WIDTH), jnp.float32, 0.0, math.log(10.0)))
    base = jax.random.normal(first, (BATCH_SEQUENCES, SEQUENCE_LENGTH, MODEL_WIDTH), jnp.float32)
    base = jnp.clip(base, -6.0, 6.0)
    return (0.1 * base * row_scale * column_scale).astype(jnp.bfloat16)


def plant(array, key, least, top_value):
    extent = array.shape
    spot = [jax.random.randint(jax.random.fold_in(key, axis), (), 0, extent[axis]) for axis in range(len(extent))]
    array = array.at[tuple(spot)].set(least)
    longest = extent.index(max(extent))
    spot[longest] = (spot[longest] + 1) % extent[longest]
    return array.at[tuple(spot)].set(top_value)


def steps_of(stream_key, shape, cuts, least, top_value):
    def one(position, parts):
        steps = jax.random.uniform(jax.random.fold_in(jax.random.fold_in(stream_key, 6), position), (parts,), jnp.float32, least / len(cuts), top_value / len(cuts))
        return jnp.repeat(jnp.exp(steps), shape[position] // parts).reshape((-1,) + (1,) * (len(shape) - position - 1))

    loudness = one(*cuts[0])
    for cut in cuts[1:]:
        loudness = loudness * one(*cut)
    return loudness


def split_up(number_of, total, reach, slope):
    portions = [(1 << 20) // math.isqrt(rank ** slope) + 1 for rank in range(2, number_of + 1)]
    spare, counts = total - reach - (number_of - 1), [1] * (number_of - 1)
    while spare > 0:
        movable = [i for i in range(number_of - 1) if counts[i] < reach]
        mass, remaining = sum([portions[i] for i in movable]), spare
        for i in movable:
            extra = min(reach - counts[i], max(1, remaining * portions[i] // mass), spare)
            counts[i] = counts[i] + extra
            spare = spare - extra
    return np.array([reach] + counts)


def uneven_parts(rng, amount, total, bound, skew):
    if amount == 2:
        one = jax.random.randint(rng, (), max(1, total - bound), min(bound, total - 1) + 1)
        return jnp.stack([one, total - one])
    sizes = jnp.asarray(split_up(amount, total, bound, skew), jnp.int32)
    couples = (amount - 1) // 2
    source_of, sink = sizes[1:1 + 2 * couples:2], sizes[2:2 + 2 * couples:2]
    margin = jnp.minimum(source_of - 1, bound - sink)
    passed = jax.random.randint(jax.random.fold_in(rng, 1), (couples,), 0, 1 << 20) % (margin + 1)
    sizes = sizes.at[1:1 + 2 * couples:2].set(source_of - passed).at[2:2 + 2 * couples:2].set(sink + passed)
    return sizes[jax.random.permutation(jax.random.fold_in(rng, 2), amount)]


def noise(stream_key, extent, scale, reach, cuts=(), held_as=jnp.bfloat16):
    values = jax.random.normal(stream_key, extent, jnp.float32) * scale
    if len(cuts) > 0:
        values = steps_of(stream_key, extent, cuts, -0.22, 0.18) * values
    return jnp.clip(values, min=-reach, max=reach).astype(held_as)


def setup_inputs(seed: int = 0) -> dict:
    arg_keys = jax.random.split(jax.random.key(seed), 10)
    layer_input = draw_layer_input(jax.random.fold_in(arg_keys[9], 71), 0)
    queries = noise(arg_keys[1], (BATCH_SEQUENCES, SEQUENCE_LENGTH, QUERY_HEADS * HEAD_SIZE), 1.0, 6.0, ((0, 8), (1, 8), (2, 4)))
    rotated_key_states = noise(arg_keys[2], (BATCH_SEQUENCES, SEQUENCE_LENGTH, KEY_VALUE_HEADS * HEAD_SIZE), 1.0, 6.0, ((0, 8), (1, 8), (2, 4)))
    values = noise(arg_keys[3], (BATCH_SEQUENCES, SEQUENCE_LENGTH, KEY_VALUE_HEADS * HEAD_SIZE), 1.0, 6.0, ((0, 8), (1, 8), (2, 4)))
    attention_out = noise(arg_keys[4], (BATCH_SEQUENCES, SEQUENCE_LENGTH, QUERY_HEADS * HEAD_SIZE), 1.0, 6.0, ((0, 8), (1, 8), (2, 4)))
    output_grad = noise(arg_keys[5], (BATCH_SEQUENCES, SEQUENCE_LENGTH, QUERY_HEADS * HEAD_SIZE), 1.0, 6.0, ((0, 8), (1, 8), (2, 4)))
    normalizer_shift = jnp.clip(1.5 * jax.random.uniform(arg_keys[6], (QUERY_HEADS,), jnp.float32) ** steps_of(arg_keys[6], (QUERY_HEADS,), ((0, 4),), -0.2, 0.2), 0.0, 1.5)
    document_lengths = jax.vmap(lambda own: uneven_parts(own, NDOC, SEQUENCE_LENGTH, 3 * SEQUENCE_LENGTH // 4, 2))(jax.random.split(arg_keys[7], BATCH_SEQUENCES)).reshape((BATCH_SEQUENCES, NDOC)).astype(jnp.int32)
    dither = plant(jax.random.randint(arg_keys[8], (2, MODEL_WIDTH, KEY_VALUE_HEADS * HEAD_SIZE), 0, 256), jax.random.fold_in(arg_keys[8], 1), 0, 255).astype(jnp.int32)
    return dict(layer_input=layer_input, queries=queries, rotated_key_states=rotated_key_states, values=values, attention_out=attention_out, output_grad=output_grad, normalizer_shift=normalizer_shift, document_lengths=document_lengths, dither=dither)


def document_tables(lengths_row, positions):
    boundary = jnp.cumsum(lengths_row).astype(jnp.int32)
    document = jnp.sum((positions[:, None] >= boundary[None, :]).astype(jnp.int32), axis=1).astype(jnp.int32)
    opening = jnp.max(jnp.where(boundary[None, :] <= positions[:, None], boundary[None, :], 0), axis=1).astype(jnp.int32)
    return document, opening


def rounded(packed_array):
    return lax.optimization_barrier(packed_array.astype(jnp.bfloat16)).astype(jnp.float32)


def group_grads(query_group, key_group, value_group, output_group, grad_group, log_norm, allowed):
    softmax_scale = HEAD_SIZE ** -0.5
    scores = jnp.einsum("trd,sd->rts", query_group, key_group) * softmax_scale
    probabilities = jnp.where(allowed[None], jnp.exp(scores - log_norm[:, :, None]), 0.0)
    value_portion = jnp.einsum("rts,trd->sd", rounded(probabilities), grad_group)
    prob_grad = jnp.einsum("trd,sd->rts", grad_group, value_group)
    row_delta = jnp.sum(grad_group * output_group, axis=-1).T
    score_gradient = rounded(probabilities * (prob_grad - row_delta[:, :, None]))
    query_part = jnp.einsum("rts,sd->trd", score_gradient, key_group) * softmax_scale
    key_portion = jnp.einsum("rts,trd->sd", score_gradient, query_group) * softmax_scale
    return query_part, key_portion, value_portion


def reference(layer_input, queries, rotated_key_states, values, attention_out, output_grad, normalizer_shift, document_lengths, dither):
    query_group_width = QUERY_HEADS // KEY_VALUE_HEADS
    positions = jnp.arange(SEQUENCE_LENGTH, dtype=jnp.int32)
    head_log_offset = normalizer_shift.astype(jnp.float32).reshape(KEY_VALUE_HEADS, query_group_width)

    def split_heads(packed_array):
        return packed_array.astype(jnp.float32).reshape(SEQUENCE_LENGTH, KEY_VALUE_HEADS, query_group_width, HEAD_SIZE).transpose(1, 0, 2, 3)

    def split_shared(packed_array):
        return packed_array.astype(jnp.float32).reshape(SEQUENCE_LENGTH, KEY_VALUE_HEADS, HEAD_SIZE).transpose(1, 0, 2)

    def one_sequence(operands):
        query_seq, key_seq, value_seq, output_seq, grad_seq, lengths_row = operands
        document, opening = document_tables(lengths_row, positions)
        visible = (positions - opening + 1).astype(jnp.float32)
        allowed = (positions[None, :] <= positions[:, None]) & (document[None, :] == document[:, None])

        def one_group(group_operands):
            query_group, key_group, value_group, output_group, grad_group, shift_group = group_operands
            log_norm = jnp.log(visible)[None, :] + shift_group[:, None]
            return group_grads(query_group, key_group, value_group, output_group, grad_group, log_norm, allowed)

        query_part, key_portion, value_portion = lax.map(one_group, (split_heads(query_seq), split_shared(key_seq), split_shared(value_seq), split_heads(output_seq), split_heads(grad_seq), head_log_offset))
        query_grad = query_part.transpose(1, 0, 2, 3).reshape(SEQUENCE_LENGTH, QUERY_HEADS * HEAD_SIZE).astype(jnp.bfloat16)
        key_gradient = key_portion.transpose(1, 0, 2).reshape(SEQUENCE_LENGTH, KEY_VALUE_HEADS * HEAD_SIZE).astype(jnp.bfloat16)
        value_gradient = value_portion.transpose(1, 0, 2).reshape(SEQUENCE_LENGTH, KEY_VALUE_HEADS * HEAD_SIZE).astype(jnp.bfloat16)
        return query_grad, key_gradient, value_gradient

    query_grad, key_gradient, value_gradient = lax.map(one_sequence, (queries, rotated_key_states, values, attention_out, output_grad, document_lengths))
    flattened_input = layer_input.reshape(BATCH_SEQUENCES * SEQUENCE_LENGTH, MODEL_WIDTH).T
    key_matrix = jnp.dot(flattened_input, key_gradient.reshape(BATCH_SEQUENCES * SEQUENCE_LENGTH, KEY_VALUE_HEADS * HEAD_SIZE), preferred_element_type=jnp.float32)
    value_matrix = jnp.dot(flattened_input, value_gradient.reshape(BATCH_SEQUENCES * SEQUENCE_LENGTH, KEY_VALUE_HEADS * HEAD_SIZE), preferred_element_type=jnp.float32)
    weight_gradient = jnp.stack([key_matrix, value_matrix])
    code_blocks = weight_gradient.reshape(2, MODEL_WIDTH // CODE_BLOCK_ROWS, CODE_BLOCK_ROWS, KEY_VALUE_HEADS, HEAD_SIZE)
    largest_value = jnp.max(jnp.abs(code_blocks), axis=(2, 4), keepdims=True)
    scaled_scores = (8.0 * code_blocks / (largest_value + 1e-6)).reshape(2, MODEL_WIDTH, KEY_VALUE_HEADS * HEAD_SIZE)
    weight_codes = scaled_scores + (dither.astype(jnp.float32) + 0.5) / 256.0
    return query_grad, weight_codes
```

```python
import functools
import math

import jax
import jax.numpy as jnp
from jax import lax
from jax.experimental import pallas as pl
from jax.experimental.pallas import tpu as pltpu
from jax.sharding import PartitionSpec as P

HEAD_SIZE = 128
SOFTMAX_SCALE = HEAD_SIZE ** (-0.5)
LOG2_E = math.log2(math.e)
KEY_TILE = 256
VMEM_LIMIT = 40 << 20
F32 = jnp.float32
BF16 = jnp.bfloat16

NT = (((1,), (1,)), ((), ()))
NN = (((1,), (0,)), ((), ()))
TN = (((0,), (0,)), ((), ()))


def dot(a, b, dims):
    return lax.dot_general(a, b, dims, preferred_element_type=F32)


def vmem_params():
    return pltpu.CompilerParams(vmem_limit_bytes=VMEM_LIMIT)


def opening_of(lengths_ref, position):
    total = jnp.int32(0)
    opening = jnp.zeros_like(position)
    for n in range(lengths_ref.shape[1]):
        total = total + lengths_ref[0, n]
        opening = jnp.where(total <= position, total, opening)
    return opening


def attention_body(shifts, first, last, *refs):
    blocks = len(shifts)
    rank_ref, lengths_ref, shift_ref, q_ref, do_ref, second_ref = refs[:6]
    rest = list(refs[6:])
    kv_refs = [rest.pop(0) for _ in range(blocks)]
    dq_in_ref = None if first else rest.pop(0)
    dq_ref = rest.pop(0)
    delta_out_ref = rest.pop(0) if first else None
    dkv_refs = [rest.pop(0) for _ in range(blocks)]
    acc_ref, key_t_ref, opening_ref, log_ref, dq_acc_ref = rest
    head = pl.program_id(0)
    rows = q_ref.shape[0]
    start = rank_ref[0] * rows
    first_opening = opening_of(lengths_ref, start)
    last_opening = opening_of(lengths_ref, start + rows - 1)

    @pl.when(head == 0)
    def _():
        acc_ref[...] = jnp.zeros_like(acc_ref)
        for b in range(blocks):
            key_t_ref[b] = kv_refs[b][:, :HEAD_SIZE].T
        position = start + lax.broadcasted_iota(jnp.int32, (8, rows), 1)
        opening = opening_of(lengths_ref, position)
        opening_ref[...] = opening
        log_ref[...] = jnp.log((position - opening + 1).astype(F32))

    log_norm = (log_ref[0:1, :] + shift_ref[head]) * LOG2_E
    if first:
        product = second_ref[...].astype(F32) * do_ref[...].astype(F32)
        row_delta = jnp.sum(product.T, axis=0, keepdims=True)
        delta_out_ref[0] = row_delta
        dq_acc_ref[...] = jnp.zeros_like(dq_acc_ref)
    else:
        row_delta = second_ref[0]
        dq_acc_ref[...] = dq_in_ref[0]

    def tile(b, k0, q0, masked):
        k = kv_refs[b][k0 : k0 + KEY_TILE, :HEAD_SIZE]
        v = kv_refs[b][k0 : k0 + KEY_TILE, HEAD_SIZE:]
        q = q_ref[q0:, :]
        do = do_ref[q0:, :]
        scores = dot(k, q, NT)
        probs = jnp.exp2(scores * (SOFTMAX_SCALE * LOG2_E) - log_norm[:, q0:])
        if masked:
            key = (start - shifts[b] * rows + k0) + lax.broadcasted_iota(jnp.int32, scores.shape, 0)
            allowed = key >= opening_ref[0:1, q0:]
            if shifts[b] == 0:
                query = (start + q0) + lax.broadcasted_iota(jnp.int32, scores.shape, 1)
                allowed = allowed & (key <= query)
            probs = jnp.where(allowed, probs, 0.0)
        prob_grad = dot(v, do, NT)
        score_grad = (probs * (prob_grad - row_delta[:, q0:])).astype(BF16)
        acc_ref[b, k0 : k0 + KEY_TILE, HEAD_SIZE:] += dot(probs.astype(BF16), do, NN)
        acc_ref[b, k0 : k0 + KEY_TILE, :HEAD_SIZE] += dot(score_grad, q, NN)
        dq_acc_ref[:, q0:] += dot(key_t_ref[b, :, k0 : k0 + KEY_TILE], score_grad, NN)

    for b in range(blocks):
        for k0 in range(0, rows, KEY_TILE):
            if shifts[b] == 0:
                tile(b, k0, k0, True)
                continue
            key_start = start - shifts[b] * rows + k0
            reached = (key_start >= 0) & (first_opening < key_start + KEY_TILE)
            whole = last_opening <= key_start
            pl.when(reached & whole)(functools.partial(tile, b, k0, 0, False))
            pl.when(reached & jnp.logical_not(whole))(functools.partial(tile, b, k0, 0, True))

    if last:
        dq_ref[...] = (dq_acc_ref[...] * SOFTMAX_SCALE).T.astype(BF16)
    else:
        dq_ref[0] = dq_acc_ref[...]

    @pl.when(head == pl.num_programs(0) - 1)
    def _():
        for b in range(blocks):
            dkv_refs[b][:, :HEAD_SIZE] = (acc_ref[b, :, :HEAD_SIZE] * SOFTMAX_SCALE).astype(dkv_refs[b].dtype)
            dkv_refs[b][:, HEAD_SIZE:] = acc_ref[b, :, HEAD_SIZE:].astype(dkv_refs[b].dtype)


def attention_step(shifts, first, last, rank, lengths, head_shift, q, do, second, kvs, dq):
    rows, width = q.shape
    heads = width // HEAD_SIZE
    blocks = len(shifts)
    smem = pl.BlockSpec(memory_space=pltpu.SMEM)
    head_block = pl.BlockSpec((rows, HEAD_SIZE), lambda h: (0, h))
    row_block = pl.BlockSpec((1, 1, rows), lambda h: (h, 0, 0))
    dq_block = pl.BlockSpec((1, HEAD_SIZE, rows), lambda h: (h, 0, 0))
    kv_block = pl.BlockSpec((rows, 2 * HEAD_SIZE), lambda h: (0, 0))
    in_specs = [smem, smem, smem, head_block, head_block, head_block if first else row_block]
    in_specs += [kv_block] * blocks + ([] if first else [dq_block])
    out_specs, out_shape = [], []
    if last:
        out_specs.append(head_block)
        out_shape.append(jax.ShapeDtypeStruct((rows, width), BF16))
    else:
        out_specs.append(dq_block)
        out_shape.append(jax.ShapeDtypeStruct((heads, HEAD_SIZE, rows), F32))
    if first:
        out_specs.append(row_block)
        out_shape.append(jax.ShapeDtypeStruct((heads, 1, rows), F32))
    for s in shifts:
        out_specs.append(kv_block)
        out_shape.append(jax.ShapeDtypeStruct((rows, 2 * HEAD_SIZE), F32 if s == 0 else BF16))
    pairs = heads * rows * rows * blocks
    return pl.pallas_call(
        functools.partial(attention_body, shifts, first, last),
        grid=(heads,),
        in_specs=in_specs,
        out_specs=out_specs,
        out_shape=out_shape,
        scratch_shapes=[
            pltpu.VMEM((blocks, rows, 2 * HEAD_SIZE), F32),
            pltpu.VMEM((blocks, HEAD_SIZE, rows), BF16),
            pltpu.VMEM((8, rows), jnp.int32),
            pltpu.VMEM((8, rows), F32),
            pltpu.VMEM((HEAD_SIZE, rows), F32),
        ],
        cost_estimate=pl.CostEstimate(
            flops=pairs * 10 * HEAD_SIZE, bytes_accessed=8 << 20, transcendentals=pairs
        ),
        compiler_params=vmem_params(),
        name="attention_" + "_".join(str(s) for s in shifts),
    )(rank, lengths, head_shift, q, do, second, *kvs, *([] if first else [dq]))


def product_body(count, x_ref, own_ref, *refs):
    parts, (out_ref, grad_ref) = refs[:count], refs[count:]

    @pl.when(pl.program_id(0) == 0)
    def _():
        total = own_ref[...]
        for part in parts:
            total = total + part[...].astype(F32)
        grad_ref[...] = total.astype(BF16)

    out_ref[0] = dot(grad_ref[...], x_ref[...], TN).astype(BF16)


def weight_product(features, own, parts, blocks):
    rows, width = features.shape
    cols = own.shape[1]
    whole = pl.BlockSpec((rows, cols), lambda d: (0, 0))
    return pl.pallas_call(
        functools.partial(product_body, len(parts)),
        grid=(blocks,),
        in_specs=[pl.BlockSpec((rows, width // blocks), lambda d: (0, d)), whole] + [whole] * len(parts),
        out_specs=pl.BlockSpec((1, cols, width // blocks), lambda d: (d, 0, 0)),
        out_shape=jax.ShapeDtypeStruct((blocks, cols, width // blocks), BF16),
        scratch_shapes=[pltpu.VMEM((rows, cols), BF16)],
        cost_estimate=pl.CostEstimate(
            flops=2 * rows * width * cols, bytes_accessed=12 << 20, transcendentals=0
        ),
        compiler_params=vmem_params(),
        name="weight_product",
    )(features, own, *parts)


def sum_body(x_ref, out_ref):
    total = x_ref[0].astype(F32)
    for n in range(1, x_ref.shape[0]):
        total = total + x_ref[n].astype(F32)
    width = out_ref.shape[2]
    for c in range(out_ref.shape[0]):
        out_ref[c] = total[:, c * width : (c + 1) * width].astype(BF16)


def sum_parts(x, blocks):
    n, rows, width = x.shape
    own = width // blocks
    per_step = 2
    return pl.pallas_call(
        sum_body,
        grid=(blocks // per_step,),
        in_specs=[pl.BlockSpec((n, rows, own * per_step), lambda c: (0, 0, c))],
        out_specs=pl.BlockSpec((per_step, rows, own), lambda c: (c, 0, 0)),
        out_shape=jax.ShapeDtypeStruct((blocks, rows, own), BF16),
        compiler_params=vmem_params(),
        name="part_sum",
    )(x)


def codes_body(parts_ref, dither_ref, out_ref):
    total = parts_ref[0].astype(F32)
    for n in range(1, parts_ref.shape[0]):
        total = total + parts_ref[n].astype(F32)
    for k in range(2):
        block = total[k * HEAD_SIZE : (k + 1) * HEAD_SIZE]
        largest = jnp.max(jnp.abs(block))
        scaled = 8.0 * block.T / (largest + 1e-06)
        out_ref[k] = scaled + (dither_ref[k].astype(F32) + 0.5) / 256.0


def weight_codes_of(parts, dither):
    return pl.pallas_call(
        codes_body,
        out_shape=jax.ShapeDtypeStruct(dither.shape, F32),
        compiler_params=vmem_params(),
        name="weight_codes",
    )(parts, dither)


def per_device(
    layer_input,
    queries,
    rotated_key_states,
    values,
    attention_out,
    output_grad,
    normalizer_shift,
    document_lengths,
    dither,
):
    context_size = lax.axis_size("context")
    dp_size = lax.axis_size("dp")
    rank = lax.axis_index("context").astype(jnp.int32).reshape(1)

    def send(x, by):
        pairs = [(i, (i + by) % context_size) for i in range(context_size)]
        return lax.ppermute(x, "context", pairs)

    own_kv = jnp.concatenate([rotated_key_states[0], values[0]], axis=1)
    kv = {0: own_kv}
    kv[1] = send(own_kv, 1)
    kv[6] = send(own_kv, -2)
    kv[2] = send(kv[1], 1)
    kv[5] = send(kv[6], -1)
    kv[3] = send(kv[2], 1)
    kv[4] = send(kv[5], -1)

    q, do = queries[0], output_grad[0]
    step = functools.partial(
        attention_step, rank=rank, lengths=document_lengths, head_shift=normalizer_shift, q=q, do=do
    )
    dq, delta, own = step((0,), True, False, second=attention_out[0], kvs=[kv[0]], dq=None)
    back = []
    groups = ((1,), (2, 6), (3, 5), (4,))
    for n, shifts in enumerate(groups):
        dq, *terms = step(
            shifts, False, n == len(groups) - 1, second=delta, kvs=[kv[s] for s in shifts], dq=dq
        )
        for s, term in zip(shifts, terms, strict=True):
            back.append(send(term, -s if s <= 4 else context_size - s))

    product = weight_product(layer_input[0], own, back, dp_size)
    parts = lax.all_to_all(product, "dp", 0, 0)
    parts = lax.all_to_all(sum_parts(parts, context_size), "context", 0, 0)
    weight_codes = weight_codes_of(parts, dither)
    return (dq[None], weight_codes)


def solution(mesh):
    placed = (
        P("dp", "context", None),
        P("dp", "context", "tensor"),
        P("dp", "context", "tensor"),
        P("dp", "context", "tensor"),
        P("dp", "context", "tensor"),
        P("dp", "context", "tensor"),
        P("tensor"),
        P("dp", None),
        P(None, ("dp", "context"), "tensor"),
    )
    return jax.shard_map(
        per_device,
        mesh=mesh,
        in_specs=placed,
        out_specs=(P("dp", "context", "tensor"), P(None, ("dp", "context"), "tensor")),
        check_vma=False,
    )
```

```python
import functools
import math

import jax
import jax.numpy as jnp
from jax import lax
from jax.experimental import pallas as pl
from jax.experimental.pallas import tpu as pltpu
from jax.sharding import PartitionSpec as P

HEAD_SIZE = 128
SOFTMAX_SCALE = HEAD_SIZE ** (-0.5)
LOG2_E = math.log2(math.e)
KEY_TILE = 256
HEADS_PER_STEP = 4
VMEM_LIMIT = 40 << 20
F32 = jnp.float32
BF16 = jnp.bfloat16

NT = (((1,), (1,)), ((), ()))
NN = (((1,), (0,)), ((), ()))
TN = (((0,), (0,)), ((), ()))


def dot(a, b, dims):
    return lax.dot_general(a, b, dims, preferred_element_type=F32)


def vmem_params():
    return pltpu.CompilerParams(vmem_limit_bytes=VMEM_LIMIT)


def opening_of(lengths_ref, position):
    total = jnp.int32(0)
    opening = jnp.zeros_like(position)
    for n in range(lengths_ref.shape[1]):
        total = total + lengths_ref[0, n]
        opening = jnp.where(total <= position, total, opening)
    return opening


def attention_body(shifts, first, last, *refs):
    blocks = len(shifts)
    rank_ref, lengths_ref, shift_ref, q_ref, do_ref, second_ref = refs[:6]
    rest = list(refs[6:])
    kv_refs = [rest.pop(0) for _ in range(blocks)]
    dq_in_ref = None if first else rest.pop(0)
    dq_ref = rest.pop(0)
    delta_out_ref = rest.pop(0) if first else None
    dkv_refs = [rest.pop(0) for _ in range(blocks)]
    acc_ref, key_t_ref, opening_ref, log_ref, dq_acc_ref = rest
    step = pl.program_id(0)
    rows = q_ref.shape[0]
    start = rank_ref[0] * rows
    first_opening = opening_of(lengths_ref, start)
    last_opening = opening_of(lengths_ref, start + rows - 1)

    @pl.when(step == 0)
    def _():
        acc_ref[...] = jnp.zeros_like(acc_ref)
        for b in range(blocks):
            key_t_ref[b] = kv_refs[b][:, :HEAD_SIZE].T
        position = start + lax.broadcasted_iota(jnp.int32, (8, rows), 1)
        opening = opening_of(lengths_ref, position)
        opening_ref[...] = opening
        log_ref[...] = jnp.log((position - opening + 1).astype(F32))

    log_norm, row_delta = [], []
    for j in range(HEADS_PER_STEP):
        log_norm.append((log_ref[0:1, :] + shift_ref[step * HEADS_PER_STEP + j]) * LOG2_E)
        lanes = slice(j * HEAD_SIZE, (j + 1) * HEAD_SIZE)
        if first:
            product = second_ref[:, lanes].astype(F32) * do_ref[:, lanes].astype(F32)
            row_delta.append(jnp.sum(product.T, axis=0, keepdims=True))
            delta_out_ref[j] = row_delta[j]
        else:
            row_delta.append(second_ref[j])
    dq_acc_ref[...] = jnp.zeros_like(dq_acc_ref) if first else dq_in_ref[...]

    def tile(b, k0, q0, masked):
        k = kv_refs[b][k0 : k0 + KEY_TILE, :HEAD_SIZE]
        v = kv_refs[b][k0 : k0 + KEY_TILE, HEAD_SIZE:]
        if masked:
            shape = (KEY_TILE, rows - q0)
            key = (start - shifts[b] * rows + k0) + lax.broadcasted_iota(jnp.int32, shape, 0)
            allowed = key >= opening_ref[0:1, q0:]
            if shifts[b] == 0:
                query = (start + q0) + lax.broadcasted_iota(jnp.int32, shape, 1)
                allowed = allowed & (key <= query)
        for j in range(HEADS_PER_STEP):
            q = q_ref[q0:, j * HEAD_SIZE : (j + 1) * HEAD_SIZE]
            do = do_ref[q0:, j * HEAD_SIZE : (j + 1) * HEAD_SIZE]
            scores = dot(k, q, NT)
            probs = jnp.exp2(scores * (SOFTMAX_SCALE * LOG2_E) - log_norm[j][:, q0:])
            if masked:
                probs = jnp.where(allowed, probs, 0.0)
            prob_grad = dot(v, do, NT)
            score_grad = (probs * (prob_grad - row_delta[j][:, q0:])).astype(BF16)
            acc_ref[b, k0 : k0 + KEY_TILE, HEAD_SIZE:] += dot(probs.astype(BF16), do, NN)
            acc_ref[b, k0 : k0 + KEY_TILE, :HEAD_SIZE] += dot(score_grad, q, NN)
            dq_acc_ref[j, :, q0:] += dot(key_t_ref[b, :, k0 : k0 + KEY_TILE], score_grad, NN)

    def block(b, masked):
        for k0 in range(0, rows, KEY_TILE):
            tile(b, k0, k0 if shifts[b] == 0 else 0, masked)

    for b in range(blocks):
        if shifts[b] == 0:
            block(b, True)
            continue
        key_start = start - shifts[b] * rows
        reached = (key_start >= 0) & (first_opening < key_start + rows)
        whole = last_opening <= key_start
        pl.when(reached & whole)(functools.partial(block, b, False))
        pl.when(reached & jnp.logical_not(whole))(functools.partial(block, b, True))

    if last:
        for j in range(HEADS_PER_STEP):
            total = dq_acc_ref[j] * SOFTMAX_SCALE
            dq_ref[:, j * HEAD_SIZE : (j + 1) * HEAD_SIZE] = total.T.astype(BF16)
    else:
        dq_ref[...] = dq_acc_ref[...]

    @pl.when(step == pl.num_programs(0) - 1)
    def _():
        for b in range(blocks):
            dkv_refs[b][:, :HEAD_SIZE] = (acc_ref[b, :, :HEAD_SIZE] * SOFTMAX_SCALE).astype(dkv_refs[b].dtype)
            dkv_refs[b][:, HEAD_SIZE:] = acc_ref[b, :, HEAD_SIZE:].astype(dkv_refs[b].dtype)


def attention_step(shifts, first, last, rank, lengths, head_shift, q, do, second, kvs, dq):
    rows, width = q.shape
    heads = width // HEAD_SIZE
    blocks = len(shifts)
    smem = pl.BlockSpec(memory_space=pltpu.SMEM)
    head_block = pl.BlockSpec((rows, HEADS_PER_STEP * HEAD_SIZE), lambda h: (0, h))
    row_block = pl.BlockSpec((HEADS_PER_STEP, 1, rows), lambda h: (h, 0, 0))
    dq_block = pl.BlockSpec((HEADS_PER_STEP, HEAD_SIZE, rows), lambda h: (h, 0, 0))
    kv_block = pl.BlockSpec((rows, 2 * HEAD_SIZE), lambda h: (0, 0))
    in_specs = [smem, smem, smem, head_block, head_block, head_block if first else row_block]
    in_specs += [kv_block] * blocks + ([] if first else [dq_block])
    out_specs, out_shape = [], []
    if last:
        out_specs.append(head_block)
        out_shape.append(jax.ShapeDtypeStruct((rows, width), BF16))
    else:
        out_specs.append(dq_block)
        out_shape.append(jax.ShapeDtypeStruct((heads, HEAD_SIZE, rows), F32))
    if first:
        out_specs.append(row_block)
        out_shape.append(jax.ShapeDtypeStruct((heads, 1, rows), F32))
    for s in shifts:
        out_specs.append(kv_block)
        out_shape.append(jax.ShapeDtypeStruct((rows, 2 * HEAD_SIZE), F32 if s == 0 else BF16))
    pairs = heads * rows * rows * blocks
    return pl.pallas_call(
        functools.partial(attention_body, shifts, first, last),
        grid=(heads // HEADS_PER_STEP,),
        in_specs=in_specs,
        out_specs=out_specs,
        out_shape=out_shape,
        scratch_shapes=[
            pltpu.VMEM((blocks, rows, 2 * HEAD_SIZE), F32),
            pltpu.VMEM((blocks, HEAD_SIZE, rows), BF16),
            pltpu.VMEM((8, rows), jnp.int32),
            pltpu.VMEM((8, rows), F32),
            pltpu.VMEM((HEADS_PER_STEP, HEAD_SIZE, rows), F32),
        ],
        cost_estimate=pl.CostEstimate(flops=pairs, bytes_accessed=1 << 20, transcendentals=0),
        compiler_params=vmem_params(),
        name="attention_" + "_".join(str(s) for s in shifts),
    )(rank, lengths, head_shift, q, do, second, *kvs, *([] if first else [dq]))


def early_sum_body(*refs):
    total = refs[0][...]
    for part in refs[1:-1]:
        total = total + part[...].astype(F32)
    refs[-1][...] = total


def early_sum(own, parts):
    return pl.pallas_call(
        early_sum_body,
        out_shape=jax.ShapeDtypeStruct(own.shape, F32),
        compiler_params=vmem_params(),
        name="early_sum",
    )(own, *parts)


def product_body(x_ref, sum_ref, part_ref, out_ref, grad_ref):
    @pl.when(pl.program_id(0) == 0)
    def _():
        grad_ref[...] = (sum_ref[...] + part_ref[...].astype(F32)).astype(BF16)

    out_ref[0] = dot(grad_ref[...], x_ref[...], TN).astype(BF16)


def weight_product(features, early, part, blocks):
    rows, width = features.shape
    cols = early.shape[1]
    whole = pl.BlockSpec((rows, cols), lambda d: (0, 0))
    return pl.pallas_call(
        product_body,
        grid=(blocks,),
        in_specs=[pl.BlockSpec((rows, width // blocks), lambda d: (0, d)), whole, whole],
        out_specs=pl.BlockSpec((1, cols, width // blocks), lambda d: (d, 0, 0)),
        out_shape=jax.ShapeDtypeStruct((blocks, cols, width // blocks), BF16),
        scratch_shapes=[pltpu.VMEM((rows, cols), BF16)],
        cost_estimate=pl.CostEstimate(
            flops=2 * rows * width * cols, bytes_accessed=12 << 20, transcendentals=0
        ),
        compiler_params=vmem_params(),
        name="weight_product",
    )(features, early, part)


def sum_body(x_ref, out_ref):
    total = x_ref[0].astype(F32)
    for n in range(1, x_ref.shape[0]):
        total = total + x_ref[n].astype(F32)
    width = out_ref.shape[2]
    for c in range(out_ref.shape[0]):
        out_ref[c] = total[:, c * width : (c + 1) * width].astype(BF16)


def sum_parts(x, blocks):
    n, rows, width = x.shape
    own = width // blocks
    per_step = 2
    return pl.pallas_call(
        sum_body,
        grid=(blocks // per_step,),
        in_specs=[pl.BlockSpec((n, rows, own * per_step), lambda c: (0, 0, c))],
        out_specs=pl.BlockSpec((per_step, rows, own), lambda c: (c, 0, 0)),
        out_shape=jax.ShapeDtypeStruct((blocks, rows, own), BF16),
        compiler_params=vmem_params(),
        name="part_sum",
    )(x)


def codes_body(parts_ref, dither_ref, out_ref):
    total = parts_ref[0].astype(F32)
    for n in range(1, parts_ref.shape[0]):
        total = total + parts_ref[n].astype(F32)
    for k in range(2):
        block = total[k * HEAD_SIZE : (k + 1) * HEAD_SIZE]
        largest = jnp.max(jnp.abs(block))
        scaled = 8.0 * block.T / (largest + 1e-06)
        out_ref[k] = scaled + (dither_ref[k].astype(F32) + 0.5) / 256.0


def weight_codes_of(parts, dither):
    return pl.pallas_call(
        codes_body,
        out_shape=jax.ShapeDtypeStruct(dither.shape, F32),
        compiler_params=vmem_params(),
        name="weight_codes",
    )(parts, dither)


def per_device(
    layer_input,
    queries,
    rotated_key_states,
    values,
    attention_out,
    output_grad,
    normalizer_shift,
    document_lengths,
    dither,
):
    context_size = lax.axis_size("context")
    dp_size = lax.axis_size("dp")
    rank = lax.axis_index("context").astype(jnp.int32).reshape(1)

    def send(x, by):
        pairs = [(i, (i + by) % context_size) for i in range(context_size)]
        return lax.ppermute(x, "context", pairs)

    own_kv = jnp.concatenate([rotated_key_states[0], values[0]], axis=1)
    kv = {0: own_kv, 1: send(own_kv, 1), 6: send(own_kv, -2)}

    q, do = queries[0], output_grad[0]
    step = functools.partial(
        attention_step, rank=rank, lengths=document_lengths, head_shift=normalizer_shift, q=q, do=do
    )
    dq, delta, own = step((0,), True, False, second=attention_out[0], kvs=[kv[0]], dq=None)
    kv[1], kv[6], dq = lax.optimization_barrier((kv[1], kv[6], dq))
    kv[2] = send(kv[1], 1)
    kv[5] = send(kv[6], -1)
    back = []

    def work(shifts, last, dq):
        dq, *terms = step(shifts, False, last, second=delta, kvs=[kv[s] for s in shifts], dq=dq)
        for s, term in zip(shifts, terms, strict=True):
            back.append(send(term, -s if s <= 4 else context_size - s))
        return dq

    dq = work((1,), False, dq)
    kv[2], kv[5], dq = lax.optimization_barrier((kv[2], kv[5], dq))
    kv[3] = send(kv[2], 1)
    kv[4] = send(kv[5], -1)
    dq = work((2, 6), False, dq)
    dq = work((3, 5), False, dq)
    dq = work((4,), True, dq)

    product = weight_product(layer_input[0], early_sum(own, back[:-1]), back[-1], dp_size)
    parts = lax.all_to_all(product, "dp", 0, 0)
    parts = lax.all_to_all(sum_parts(parts, context_size), "context", 0, 0)
    weight_codes = weight_codes_of(parts, dither)
    return (dq[None], weight_codes)


def solution(mesh):
    placed = (
        P("dp", "context", None),
        P("dp", "context", "tensor"),
        P("dp", "context", "tensor"),
        P("dp", "context", "tensor"),
        P("dp", "context", "tensor"),
        P("dp", "context", "tensor"),
        P("tensor"),
        P("dp", None),
        P(None, ("dp", "context"), "tensor"),
    )
    return jax.shard_map(
        per_device,
        mesh=mesh,
        in_specs=placed,
        out_specs=(P("dp", "context", "tensor"), P(None, ("dp", "context"), "tensor")),
        check_vma=False,
    )
```

```python
import functools
import math

import jax
import jax.numpy as jnp
from jax import lax
from jax.experimental import pallas as pl
from jax.experimental.pallas import tpu as pltpu
from jax.sharding import PartitionSpec as P

HEAD_SIZE = 128
SOFTMAX_SCALE = HEAD_SIZE ** (-0.5)
LOG2_E = math.log2(math.e)
KEY_TILE = 256
HEADS_PER_STEP = 4
VMEM_LIMIT = 40 << 20
F32 = jnp.float32
BF16 = jnp.bfloat16

NT = (((1,), (1,)), ((), ()))
NN = (((1,), (0,)), ((), ()))
TN = (((0,), (0,)), ((), ()))


def dot(a, b, dims):
    return lax.dot_general(a, b, dims, preferred_element_type=F32)


def vmem_params():
    return pltpu.CompilerParams(vmem_limit_bytes=VMEM_LIMIT)


def opening_of(lengths_ref, position):
    total = jnp.int32(0)
    opening = jnp.zeros_like(position)
    for n in range(lengths_ref.shape[1]):
        total = total + lengths_ref[0, n]
        opening = jnp.where(total <= position, total, opening)
    return opening


def prepare_body(
    rank_ref,
    core_ref,
    lengths_ref,
    shift_ref,
    o_ref,
    do_ref,
    features_ref,
    delta_ref,
    norm_ref,
    opening_ref,
    bounds_ref,
    parts_ref,
    sem,
):
    count, _, half = parts_ref.shape
    copies = []
    for n in range(count):
        first = pl.multiple_of((2 * n + core_ref[0]) * half, half)
        copies.append(
            pltpu.make_async_copy(features_ref.at[:, pl.ds(first, half)], parts_ref.at[n], sem.at[n])
        )
        copies[n].start()
    heads, rows = delta_ref.shape[0], delta_ref.shape[2]
    start = rank_ref[0] * rows
    bounds_ref[0] = opening_of(lengths_ref, start)
    bounds_ref[1] = opening_of(lengths_ref, start + rows - 1)
    position = start + lax.broadcasted_iota(jnp.int32, opening_ref.shape, 1)
    opening = opening_of(lengths_ref, position)
    opening_ref[...] = opening
    log_visible = jnp.log((position - opening + 1).astype(F32))[0:1, :]
    for h in range(heads):
        lanes = slice(h * HEAD_SIZE, (h + 1) * HEAD_SIZE)
        product = o_ref[:, lanes].astype(F32) * do_ref[:, lanes].astype(F32)
        delta_ref[h] = jnp.sum(product.T, axis=0, keepdims=True)
        norm_ref[h] = (log_visible + shift_ref[h]) * LOG2_E
    for copy in copies:
        copy.wait()


def prepare(rank, core, lengths, head_shift, o, do, features, parts):
    rows, width = o.shape
    heads = width // HEAD_SIZE
    smem = pl.BlockSpec(memory_space=pltpu.SMEM)
    vmem = pl.BlockSpec(memory_space=pltpu.VMEM)
    return pl.pallas_call(
        prepare_body,
        in_specs=[smem, smem, smem, smem, vmem, vmem, pl.BlockSpec(memory_space=pltpu.HBM)],
        out_specs=[vmem, vmem, vmem, smem, pl.BlockSpec(memory_space=pltpu.HBM)],
        out_shape=[
            jax.ShapeDtypeStruct((heads, 1, rows), F32),
            jax.ShapeDtypeStruct((heads, 1, rows), F32),
            jax.ShapeDtypeStruct((8, rows), jnp.int32),
            jax.ShapeDtypeStruct((2,), jnp.int32),
            jax.ShapeDtypeStruct((parts, rows, features.shape[1] // parts // 2), BF16),
        ],
        scratch_shapes=[pltpu.SemaphoreType.DMA((parts,))],
        compiler_params=vmem_params(),
        name="prepare",
    )(rank, core, lengths, head_shift, o, do, features)


def attention_body(shifts, first, last, *refs):
    blocks = len(shifts)
    rank_ref, bounds_ref, q_ref, do_ref, delta_ref, norm_ref, opening_ref = refs[:7]
    rest = list(refs[7:])
    kv_refs = [rest.pop(0) for _ in range(blocks)]
    dq_in_ref = None if first else rest.pop(0)
    dq_ref = rest.pop(0)
    dkv_refs = [rest.pop(0) for _ in range(blocks)]
    acc_ref, key_t_ref, dq_acc_ref = rest
    step = pl.program_id(0)
    rows = q_ref.shape[0]
    start = rank_ref[0] * rows
    first_opening, last_opening = bounds_ref[0], bounds_ref[1]

    @pl.when(step == 0)
    def _():
        acc_ref[...] = jnp.zeros_like(acc_ref)
        for b in range(blocks):
            key_t_ref[b] = kv_refs[b][:, :HEAD_SIZE].T

    dq_acc_ref[...] = jnp.zeros_like(dq_acc_ref) if first else dq_in_ref[...]

    def tile(b, k0, q0, masked):
        k = kv_refs[b][k0 : k0 + KEY_TILE, :HEAD_SIZE]
        v = kv_refs[b][k0 : k0 + KEY_TILE, HEAD_SIZE:]
        if masked:
            shape = (KEY_TILE, rows - q0)
            key = (start - shifts[b] * rows + k0) + lax.broadcasted_iota(jnp.int32, shape, 0)
            allowed = key >= opening_ref[0:1, q0:]
            if shifts[b] == 0:
                query = (start + q0) + lax.broadcasted_iota(jnp.int32, shape, 1)
                allowed = allowed & (key <= query)
        for j in range(HEADS_PER_STEP):
            q = q_ref[q0:, j * HEAD_SIZE : (j + 1) * HEAD_SIZE]
            do = do_ref[q0:, j * HEAD_SIZE : (j + 1) * HEAD_SIZE]
            scores = dot(k, q, NT)
            probs = jnp.exp2(scores * (SOFTMAX_SCALE * LOG2_E) - norm_ref[j, :, q0:])
            if masked:
                probs = jnp.where(allowed, probs, 0.0)
            prob_grad = dot(v, do, NT)
            score_grad = (probs * (prob_grad - delta_ref[j, :, q0:])).astype(BF16)
            acc_ref[b, k0 : k0 + KEY_TILE, HEAD_SIZE:] += dot(probs.astype(BF16), do, NN)
            acc_ref[b, k0 : k0 + KEY_TILE, :HEAD_SIZE] += dot(score_grad, q, NN)
            dq_acc_ref[j, :, q0:] += dot(key_t_ref[b, :, k0 : k0 + KEY_TILE], score_grad, NN)

    def block(b, masked):
        for k0 in range(0, rows, KEY_TILE):
            tile(b, k0, k0 if shifts[b] == 0 else 0, masked)

    for b in range(blocks):
        if shifts[b] == 0:
            block(b, True)
            continue
        key_start = start - shifts[b] * rows
        reached = (key_start >= 0) & (first_opening < key_start + rows)
        whole = last_opening <= key_start
        pl.when(reached & whole)(functools.partial(block, b, False))
        pl.when(reached & jnp.logical_not(whole))(functools.partial(block, b, True))

    if last:
        for j in range(HEADS_PER_STEP):
            total = dq_acc_ref[j] * SOFTMAX_SCALE
            dq_ref[:, j * HEAD_SIZE : (j + 1) * HEAD_SIZE] = total.T.astype(BF16)
    else:
        dq_ref[...] = dq_acc_ref[...]

    @pl.when(step == pl.num_programs(0) - 1)
    def _():
        for b in range(blocks):
            dkv_refs[b][:, :HEAD_SIZE] = (acc_ref[b, :, :HEAD_SIZE] * SOFTMAX_SCALE).astype(dkv_refs[b].dtype)
            dkv_refs[b][:, HEAD_SIZE:] = acc_ref[b, :, HEAD_SIZE:].astype(dkv_refs[b].dtype)


def attention_step(shifts, first, last, rank, bounds, q, do, delta, norm, opening, kvs, dq):
    rows, width = q.shape
    heads = width // HEAD_SIZE
    blocks = len(shifts)
    smem = pl.BlockSpec(memory_space=pltpu.SMEM)
    head_block = pl.BlockSpec((rows, HEADS_PER_STEP * HEAD_SIZE), lambda h: (0, h))
    row_block = pl.BlockSpec((HEADS_PER_STEP, 1, rows), lambda h: (h, 0, 0))
    dq_block = pl.BlockSpec((HEADS_PER_STEP, HEAD_SIZE, rows), lambda h: (h, 0, 0))
    kv_block = pl.BlockSpec((rows, 2 * HEAD_SIZE), lambda h: (0, 0))
    opening_block = pl.BlockSpec(opening.shape, lambda h: (0, 0))
    in_specs = [smem, smem, head_block, head_block, row_block, row_block, opening_block]
    in_specs += [kv_block] * blocks + ([] if first else [dq_block])
    if last:
        out_specs = [head_block]
        out_shape = [jax.ShapeDtypeStruct((rows, width), BF16)]
    else:
        out_specs = [dq_block]
        out_shape = [jax.ShapeDtypeStruct((heads, HEAD_SIZE, rows), F32)]
    for s in shifts:
        out_specs.append(kv_block)
        out_shape.append(jax.ShapeDtypeStruct((rows, 2 * HEAD_SIZE), F32 if s == 0 else BF16))
    pairs = heads * rows * rows * blocks
    return pl.pallas_call(
        functools.partial(attention_body, shifts, first, last),
        grid=(heads // HEADS_PER_STEP,),
        in_specs=in_specs,
        out_specs=out_specs,
        out_shape=out_shape,
        scratch_shapes=[
            pltpu.VMEM((blocks, rows, 2 * HEAD_SIZE), F32),
            pltpu.VMEM((blocks, HEAD_SIZE, rows), BF16),
            pltpu.VMEM((HEADS_PER_STEP, HEAD_SIZE, rows), F32),
        ],
        cost_estimate=pl.CostEstimate(flops=pairs, bytes_accessed=1 << 20, transcendentals=0),
        compiler_params=vmem_params(),
        name="attention_" + "_".join(str(s) for s in shifts),
    )(rank, bounds, q, do, delta, norm, opening, *kvs, *([] if first else [dq]))


def early_sum_body(*refs):
    total = refs[0][...]
    for part in refs[1:-1]:
        total = total + part[...].astype(F32)
    refs[-1][...] = total


def early_sum(own, parts):
    return pl.pallas_call(
        early_sum_body,
        out_shape=jax.ShapeDtypeStruct(own.shape, F32),
        compiler_params=vmem_params(),
        name="early_sum",
    )(own, *parts)


def share_body(early_ref, part_ref, out_ref):
    total = (early_ref[...] + part_ref[...].astype(F32)).astype(BF16)
    for n in range(out_ref.shape[0]):
        out_ref[n] = total


def share_copies(early, part, copies):
    return pl.pallas_call(
        share_body,
        out_shape=jax.ShapeDtypeStruct((copies,) + early.shape, BF16),
        compiler_params=vmem_params(),
        name="share_copies",
    )(early, part)


def product_body(core_ref, own_ref, other_ref, grad_ref, out_ref, acc_ref):
    step = pl.program_id(0)

    @pl.when(step == 0)
    def _():
        acc_ref[...] = jnp.zeros_like(acc_ref)

    grad = grad_ref[...].reshape(-1, grad_ref.shape[2])
    acc_ref[0] += dot(grad, own_ref[...].reshape(-1, own_ref.shape[2]), TN)
    acc_ref[1] += dot(grad, other_ref[...].reshape(-1, other_ref.shape[2]), TN)

    @pl.when(step == pl.num_programs(0) - 1)
    def _():
        low = acc_ref[core_ref[0]].astype(BF16)
        high = acc_ref[1 - core_ref[0]].astype(BF16)
        width = out_ref.shape[2]
        per_half = out_ref.shape[0] // 2
        for c in range(per_half):
            out_ref[c] = low[:, c * width : (c + 1) * width]
            out_ref[per_half + c] = high[:, c * width : (c + 1) * width]


def weight_product(core, own_half, other_half, grads, blocks):
    parts, rows, half = own_half.shape
    cols = grads.shape[2]
    width = 2 * half // blocks
    per_step = 2
    half_block = pl.BlockSpec((per_step, rows, half), lambda d: (d, 0, 0))
    return pl.pallas_call(
        product_body,
        grid=(parts // per_step,),
        in_specs=[
            pl.BlockSpec(memory_space=pltpu.SMEM),
            half_block,
            half_block,
            pl.BlockSpec((per_step, rows, cols), lambda d: (d, 0, 0)),
        ],
        out_specs=pl.BlockSpec((blocks, cols, width), lambda d: (0, 0, 0)),
        out_shape=jax.ShapeDtypeStruct((blocks, cols, width), BF16),
        scratch_shapes=[pltpu.VMEM((2, cols, half), F32)],
        compiler_params=vmem_params(),
        name="weight_product",
    )(core, own_half, other_half, grads)


def codes_body(parts_ref, dither_ref, out_ref):
    total = parts_ref[0].astype(F32)
    for n in range(1, parts_ref.shape[0]):
        total = total + parts_ref[n].astype(F32)
    for k in range(2):
        block = total[k * HEAD_SIZE : (k + 1) * HEAD_SIZE]
        largest = jnp.max(jnp.abs(block))
        scaled = 8.0 * block.T / (largest + 1e-06)
        out_ref[k] = scaled + (dither_ref[k].astype(F32) + 0.5) / 256.0


def weight_codes_of(parts, dither):
    return pl.pallas_call(
        codes_body,
        out_shape=jax.ShapeDtypeStruct(dither.shape, F32),
        compiler_params=vmem_params(),
        name="weight_codes",
    )(parts, dither)


def per_device(
    layer_input,
    queries,
    rotated_key_states,
    values,
    attention_out,
    output_grad,
    normalizer_shift,
    document_lengths,
    dither,
):
    context_size = lax.axis_size("context")
    dp_size = lax.axis_size("dp")
    rank = lax.axis_index("context").astype(jnp.int32).reshape(1)

    def send(x, by, sources=range(context_size)):
        return lax.ppermute(x, "context", [(i, (i + by) % context_size) for i in sources])

    def give_back(x, by):
        return send(x, -by, range(by, context_size))

    own_kv = jnp.concatenate([rotated_key_states[0], values[0]], axis=1)
    kv = {1: send(own_kv, 1), 6: send(own_kv, -2)}

    q, do = queries[0], output_grad[0]
    core = (lax.axis_index("tensor") % 2).astype(jnp.int32).reshape(1)
    delta, norm, opening, bounds, features = prepare(
        rank, core, document_lengths, normalizer_shift, attention_out[0], do, layer_input[0], dp_size
    )
    kv[1], kv[6], delta, features = lax.optimization_barrier((kv[1], kv[6], delta, features))
    own_half = lax.all_to_all(features, "dp", 0, 0)
    step = functools.partial(
        attention_step, rank=rank, bounds=bounds, q=q, do=do, delta=delta, norm=norm, opening=opening
    )
    back = []
    kv[2] = send(kv[1], 1)
    dq, term = step((1,), True, False, kvs=[kv[1]], dq=None)
    back.append(give_back(term, 1))
    kv[2], kv[6], dq = lax.optimization_barrier((kv[2], kv[6], dq))
    kv[3] = send(kv[2], 1)
    kv[5] = send(kv[6], -1)

    def work(shifts, dq):
        dq, *terms = step(shifts, False, False, kvs=[kv[s] for s in shifts], dq=dq)
        return dq, [give_back(term, s) for s, term in zip(shifts, terms, strict=True)]

    dq, terms = work((2, 6), dq)
    back += terms
    kv[3], kv[5], dq = lax.optimization_barrier((kv[3], kv[5], dq))
    kv[4] = send(kv[3], 1, range(3, context_size - 1))
    dq, middle = work((3, 5), dq)
    dq, back = lax.optimization_barrier((dq, back))
    dq, (last,) = work((4,), dq)
    dq, middle, own_half = lax.optimization_barrier((dq, middle, own_half))
    swap = [(t, t ^ 1) for t in range(lax.axis_size("tensor"))]
    other_half = lax.ppermute(own_half, "tensor", swap)
    dq, own = step((0,), False, True, kvs=[own_kv], dq=dq)
    back += middle + [last]

    grads = share_copies(early_sum(own, back[:-1]), back[-1], dp_size)
    grads = lax.all_to_all(grads, "dp", 0, 0)
    product = weight_product(core, own_half, other_half, grads, context_size)
    parts = lax.all_to_all(product, "context", 0, 0)
    weight_codes = weight_codes_of(parts, dither)
    return (dq[None], weight_codes)


def solution(mesh):
    placed = (
        P("dp", "context", None),
        P("dp", "context", "tensor"),
        P("dp", "context", "tensor"),
        P("dp", "context", "tensor"),
        P("dp", "context", "tensor"),
        P("dp", "context", "tensor"),
        P("tensor"),
        P("dp", None),
        P(None, ("dp", "context"), "tensor"),
    )
    return jax.shard_map(
        per_device,
        mesh=mesh,
        in_specs=placed,
        out_specs=(P("dp", "context", "tensor"), P(None, ("dp", "context"), "tensor")),
        check_vma=False,
    )
```

```python
import functools
import math

import jax
import jax.numpy as jnp
from jax import lax
from jax.experimental import pallas as pl
from jax.experimental.pallas import tpu as pltpu
from jax.sharding import PartitionSpec as P

HEAD_SIZE = 128
SOFTMAX_SCALE = HEAD_SIZE ** (-0.5)
LOG2_E = math.log2(math.e)
KEY_TILE = 256
HEADS_PER_STEP = 4
VMEM_LIMIT = 40 << 20
F32 = jnp.float32
BF16 = jnp.bfloat16

NT = (((1,), (1,)), ((), ()))
NN = (((1,), (0,)), ((), ()))
TN = (((0,), (0,)), ((), ()))


def dot(a, b, dims):
    return lax.dot_general(a, b, dims, preferred_element_type=F32)


def vmem_params():
    return pltpu.CompilerParams(vmem_limit_bytes=VMEM_LIMIT)


def opening_of(lengths_ref, position):
    total = jnp.int32(0)
    opening = jnp.zeros_like(position)
    for n in range(lengths_ref.shape[1]):
        total = total + lengths_ref[0, n]
        opening = jnp.where(total <= position, total, opening)
    return opening


def prepare_body(
    rank_ref,
    core_ref,
    lengths_ref,
    shift_ref,
    o_ref,
    do_ref,
    features_ref,
    delta_ref,
    norm_ref,
    opening_ref,
    bounds_ref,
    parts_ref,
    sem,
):
    count, _, half = parts_ref.shape
    copies = []
    for n in range(count):
        first = pl.multiple_of((2 * n + core_ref[0]) * half, half)
        copies.append(
            pltpu.make_async_copy(features_ref.at[:, pl.ds(first, half)], parts_ref.at[n], sem.at[n])
        )
        copies[n].start()
    heads, rows = delta_ref.shape[0], delta_ref.shape[2]
    start = rank_ref[0] * rows
    bounds_ref[0] = opening_of(lengths_ref, start)
    bounds_ref[1] = opening_of(lengths_ref, start + rows - 1)
    position = start + lax.broadcasted_iota(jnp.int32, opening_ref.shape, 1)
    opening = opening_of(lengths_ref, position)
    opening_ref[...] = opening
    log_visible = jnp.log((position - opening + 1).astype(F32))[0:1, :]
    for h in range(heads):
        lanes = slice(h * HEAD_SIZE, (h + 1) * HEAD_SIZE)
        product = o_ref[:, lanes].astype(F32) * do_ref[:, lanes].astype(F32)
        delta_ref[h] = jnp.sum(product.T, axis=0, keepdims=True)
        norm_ref[h] = (log_visible + shift_ref[h]) * LOG2_E
    for copy in copies:
        copy.wait()


def prepare(rank, core, lengths, head_shift, o, do, features, parts):
    rows, width = o.shape
    heads = width // HEAD_SIZE
    smem = pl.BlockSpec(memory_space=pltpu.SMEM)
    vmem = pl.BlockSpec(memory_space=pltpu.VMEM)
    return pl.pallas_call(
        prepare_body,
        in_specs=[smem, smem, smem, smem, vmem, vmem, pl.BlockSpec(memory_space=pltpu.HBM)],
        out_specs=[vmem, vmem, vmem, smem, pl.BlockSpec(memory_space=pltpu.HBM)],
        out_shape=[
            jax.ShapeDtypeStruct((heads, 1, rows), F32),
            jax.ShapeDtypeStruct((heads, 1, rows), F32),
            jax.ShapeDtypeStruct((8, rows), jnp.int32),
            jax.ShapeDtypeStruct((2,), jnp.int32),
            jax.ShapeDtypeStruct((parts, rows, features.shape[1] // parts // 2), BF16),
        ],
        scratch_shapes=[pltpu.SemaphoreType.DMA((parts,))],
        compiler_params=vmem_params(),
        name="prepare",
    )(rank, core, lengths, head_shift, o, do, features)


def attention_body(shifts, first, last, *refs):
    blocks = len(shifts)
    rank_ref, bounds_ref, q_ref, do_ref, delta_ref, norm_ref, opening_ref = refs[:7]
    rest = list(refs[7:])
    kv_refs = [rest.pop(0) for _ in range(blocks)]
    dq_in_ref = None if first else rest.pop(0)
    dq_ref = rest.pop(0)
    dkv_refs = [rest.pop(0) for _ in range(blocks)]
    acc_ref, key_t_ref, dq_acc_ref = rest
    step = pl.program_id(0)
    rows = q_ref.shape[0]
    start = rank_ref[0] * rows
    first_opening, last_opening = bounds_ref[0], bounds_ref[1]

    @pl.when(step == 0)
    def _():
        acc_ref[...] = jnp.zeros_like(acc_ref)
        for b in range(blocks):
            key_t_ref[b] = kv_refs[b][:, :HEAD_SIZE].T

    dq_acc_ref[...] = jnp.zeros_like(dq_acc_ref) if first else dq_in_ref[...]

    def tile(b, k0, q0, masked):
        k = kv_refs[b][k0 : k0 + KEY_TILE, :HEAD_SIZE]
        v = kv_refs[b][k0 : k0 + KEY_TILE, HEAD_SIZE:]
        if masked:
            shape = (KEY_TILE, rows - q0)
            key = (start - shifts[b] * rows + k0) + lax.broadcasted_iota(jnp.int32, shape, 0)
            allowed = key >= opening_ref[0:1, q0:]
            if shifts[b] == 0:
                query = (start + q0) + lax.broadcasted_iota(jnp.int32, shape, 1)
                allowed = allowed & (key <= query)
        for j in range(HEADS_PER_STEP):
            q = q_ref[q0:, j * HEAD_SIZE : (j + 1) * HEAD_SIZE]
            do = do_ref[q0:, j * HEAD_SIZE : (j + 1) * HEAD_SIZE]
            scores = dot(k, q, NT)
            probs = jnp.exp2(scores * (SOFTMAX_SCALE * LOG2_E) - norm_ref[j, :, q0:])
            if masked:
                probs = jnp.where(allowed, probs, 0.0)
            prob_grad = dot(v, do, NT)
            score_grad = (probs * (prob_grad - delta_ref[j, :, q0:])).astype(BF16)
            acc_ref[b, k0 : k0 + KEY_TILE, HEAD_SIZE:] += dot(probs.astype(BF16), do, NN)
            acc_ref[b, k0 : k0 + KEY_TILE, :HEAD_SIZE] += dot(score_grad, q, NN)
            dq_acc_ref[j, :, q0:] += dot(key_t_ref[b, :, k0 : k0 + KEY_TILE], score_grad, NN)

    def block(b, masked):
        for k0 in range(0, rows, KEY_TILE):
            tile(b, k0, k0 if shifts[b] == 0 else 0, masked)

    for b in range(blocks):
        if shifts[b] == 0:
            block(b, True)
            continue
        key_start = start - shifts[b] * rows
        reached = (key_start >= 0) & (first_opening < key_start + rows)
        whole = last_opening <= key_start
        pl.when(reached & whole)(functools.partial(block, b, False))
        pl.when(reached & jnp.logical_not(whole))(functools.partial(block, b, True))

    if last:
        for j in range(HEADS_PER_STEP):
            total = dq_acc_ref[j] * SOFTMAX_SCALE
            dq_ref[:, j * HEAD_SIZE : (j + 1) * HEAD_SIZE] = total.T.astype(BF16)
    else:
        dq_ref[...] = dq_acc_ref[...]

    @pl.when(step == pl.num_programs(0) - 1)
    def _():
        for b in range(blocks):
            dkv_refs[b][:, :HEAD_SIZE] = (acc_ref[b, :, :HEAD_SIZE] * SOFTMAX_SCALE).astype(dkv_refs[b].dtype)
            dkv_refs[b][:, HEAD_SIZE:] = acc_ref[b, :, HEAD_SIZE:].astype(dkv_refs[b].dtype)


def attention_step(shifts, first, last, rank, bounds, q, do, delta, norm, opening, kvs, dq):
    rows, width = q.shape
    heads = width // HEAD_SIZE
    blocks = len(shifts)
    smem = pl.BlockSpec(memory_space=pltpu.SMEM)
    head_block = pl.BlockSpec((rows, HEADS_PER_STEP * HEAD_SIZE), lambda h: (0, h))
    row_block = pl.BlockSpec((HEADS_PER_STEP, 1, rows), lambda h: (h, 0, 0))
    dq_block = pl.BlockSpec((HEADS_PER_STEP, HEAD_SIZE, rows), lambda h: (h, 0, 0))
    kv_block = pl.BlockSpec((rows, 2 * HEAD_SIZE), lambda h: (0, 0))
    opening_block = pl.BlockSpec(opening.shape, lambda h: (0, 0))
    in_specs = [smem, smem, head_block, head_block, row_block, row_block, opening_block]
    in_specs += [kv_block] * blocks + ([] if first else [dq_block])
    if last:
        out_specs = [head_block]
        out_shape = [jax.ShapeDtypeStruct((rows, width), BF16)]
    else:
        out_specs = [dq_block]
        out_shape = [jax.ShapeDtypeStruct((heads, HEAD_SIZE, rows), F32)]
    for s in shifts:
        out_specs.append(kv_block)
        out_shape.append(jax.ShapeDtypeStruct((rows, 2 * HEAD_SIZE), F32 if s == 0 else BF16))
    pairs = heads * rows * rows * blocks
    return pl.pallas_call(
        functools.partial(attention_body, shifts, first, last),
        grid=(heads // HEADS_PER_STEP,),
        in_specs=in_specs,
        out_specs=out_specs,
        out_shape=out_shape,
        scratch_shapes=[
            pltpu.VMEM((blocks, rows, 2 * HEAD_SIZE), F32),
            pltpu.VMEM((blocks, HEAD_SIZE, rows), BF16),
            pltpu.VMEM((HEADS_PER_STEP, HEAD_SIZE, rows), F32),
        ],
        cost_estimate=pl.CostEstimate(flops=pairs, bytes_accessed=1 << 20, transcendentals=0),
        compiler_params=vmem_params(),
        name="attention_" + "_".join(str(s) for s in shifts),
    )(rank, bounds, q, do, delta, norm, opening, *kvs, *([] if first else [dq]))


def early_sum_body(*refs):
    total = refs[0][...]
    for part in refs[1:-1]:
        total = total + part[...].astype(F32)
    refs[-1][...] = total


def early_sum(own, parts):
    return pl.pallas_call(
        early_sum_body,
        out_shape=jax.ShapeDtypeStruct(own.shape, F32),
        compiler_params=vmem_params(),
        name="early_sum",
    )(own, *parts)


def share_body(early_ref, part_ref, out_ref):
    total = (early_ref[...] + part_ref[...].astype(F32)).astype(BF16)
    for n in range(out_ref.shape[0]):
        out_ref[n] = total


def share_copies(early, part, copies):
    return pl.pallas_call(
        share_body,
        out_shape=jax.ShapeDtypeStruct((copies,) + early.shape, BF16),
        compiler_params=vmem_params(),
        name="share_copies",
    )(early, part)


def product_body(core_ref, own_ref, other_ref, grad_ref, out_ref, acc_ref):
    step = pl.program_id(0)

    @pl.when(step == 0)
    def _():
        acc_ref[...] = jnp.zeros_like(acc_ref)

    grad = grad_ref[...].reshape(-1, grad_ref.shape[2])
    acc_ref[0] += dot(grad, own_ref[...].reshape(-1, own_ref.shape[2]), TN)
    acc_ref[1] += dot(grad, other_ref[...].reshape(-1, other_ref.shape[2]), TN)

    @pl.when(step == pl.num_programs(0) - 1)
    def _():
        low = acc_ref[core_ref[0]].astype(BF16)
        high = acc_ref[1 - core_ref[0]].astype(BF16)
        width = out_ref.shape[2]
        per_half = out_ref.shape[0] // 2
        for c in range(per_half):
            out_ref[c] = low[:, c * width : (c + 1) * width]
            out_ref[per_half + c] = high[:, c * width : (c + 1) * width]


def weight_product(core, own_half, other_half, grads, blocks):
    parts, rows, half = own_half.shape
    cols = grads.shape[2]
    width = 2 * half // blocks
    per_step = 2
    half_block = pl.BlockSpec((per_step, rows, half), lambda d: (d, 0, 0))
    return pl.pallas_call(
        product_body,
        grid=(parts // per_step,),
        in_specs=[
            pl.BlockSpec(memory_space=pltpu.SMEM),
            half_block,
            half_block,
            pl.BlockSpec((per_step, rows, cols), lambda d: (d, 0, 0)),
        ],
        out_specs=pl.BlockSpec((blocks, cols, width), lambda d: (0, 0, 0)),
        out_shape=jax.ShapeDtypeStruct((blocks, cols, width), BF16),
        scratch_shapes=[pltpu.VMEM((2, cols, half), F32)],
        compiler_params=vmem_params(),
        name="weight_product",
    )(core, own_half, other_half, grads)


def codes_body(parts_ref, dither_ref, out_ref):
    total = parts_ref[0].astype(F32)
    for n in range(1, parts_ref.shape[0]):
        total = total + parts_ref[n].astype(F32)
    for k in range(2):
        block = total[k * HEAD_SIZE : (k + 1) * HEAD_SIZE]
        largest = jnp.max(jnp.abs(block))
        scaled = 8.0 * block.T / (largest + 1e-06)
        out_ref[k] = scaled + (dither_ref[k].astype(F32) + 0.5) / 256.0


def weight_codes_of(parts, dither):
    return pl.pallas_call(
        codes_body,
        out_shape=jax.ShapeDtypeStruct(dither.shape, F32),
        compiler_params=vmem_params(),
        name="weight_codes",
    )(parts, dither)


def per_device(
    layer_input,
    queries,
    rotated_key_states,
    values,
    attention_out,
    output_grad,
    normalizer_shift,
    document_lengths,
    dither,
):
    context_size = lax.axis_size("context")
    dp_size = lax.axis_size("dp")
    rank = lax.axis_index("context").astype(jnp.int32).reshape(1)

    def send(x, by, sources=range(context_size)):
        return lax.ppermute(x, "context", [(i, (i + by) % context_size) for i in sources])

    def give_back(x, by):
        return send(x, -by, range(by, context_size))

    own_kv = jnp.concatenate([rotated_key_states[0], values[0]], axis=1)
    kv = {1: send(own_kv, 1), 6: send(own_kv, -2)}

    q, do = queries[0], output_grad[0]
    core = (lax.axis_index("tensor") % 2).astype(jnp.int32).reshape(1)
    delta, norm, opening, bounds, features = prepare(
        rank, core, document_lengths, normalizer_shift, attention_out[0], do, layer_input[0], dp_size
    )
    kv[1], kv[6], delta, features = lax.optimization_barrier((kv[1], kv[6], delta, features))
    own_half = lax.all_to_all(features, "dp", 0, 0)
    step = functools.partial(
        attention_step, rank=rank, bounds=bounds, q=q, do=do, delta=delta, norm=norm, opening=opening
    )
    back = []
    kv[2] = send(kv[1], 1)
    dq, term = step((1,), True, False, kvs=[kv[1]], dq=None)
    back.append(give_back(term, 1))
    kv[2], kv[6], dq = lax.optimization_barrier((kv[2], kv[6], dq))
    kv[3] = send(kv[2], 1)
    kv[5] = send(kv[6], -1)

    def work(shifts, dq):
        dq, *terms = step(shifts, False, False, kvs=[kv[s] for s in shifts], dq=dq)
        return dq, [give_back(term, s) for s, term in zip(shifts, terms, strict=True)]

    dq, terms = work((2, 6), dq)
    back += terms
    kv[3], kv[5], dq = lax.optimization_barrier((kv[3], kv[5], dq))
    kv[4] = send(kv[3], 1, range(3, context_size - 1))
    dq, middle = work((3, 5), dq)
    back += middle
    dq, (last,) = work((4,), dq)
    dq, own = step((0,), False, True, kvs=[own_kv], dq=dq)

    grads = share_copies(early_sum(own, back), last, dp_size)
    own_half, grads = lax.optimization_barrier((own_half, grads))
    swap = [(t, t ^ 1) for t in range(lax.axis_size("tensor"))]
    other_half = lax.ppermute(own_half, "tensor", swap)
    grads = lax.all_to_all(grads, "dp", 0, 0)
    product = weight_product(core, own_half, other_half, grads, context_size)
    parts = lax.all_to_all(product, "context", 0, 0)
    weight_codes = weight_codes_of(parts, dither)
    return (dq[None], weight_codes)


def solution(mesh):
    placed = (
        P("dp", "context", None),
        P("dp", "context", "tensor"),
        P("dp", "context", "tensor"),
        P("dp", "context", "tensor"),
        P("dp", "context", "tensor"),
        P("dp", "context", "tensor"),
        P("tensor"),
        P("dp", None),
        P(None, ("dp", "context"), "tensor"),
    )
    return jax.shard_map(
        per_device,
        mesh=mesh,
        in_specs=placed,
        out_specs=(P("dp", "context", "tensor"), P(None, ("dp", "context"), "tensor")),
        check_vma=False,
    )
```

```python
import functools
import math

import jax
import jax.numpy as jnp
from jax import lax
from jax.experimental import pallas as pl
from jax.experimental.pallas import tpu as pltpu
from jax.sharding import PartitionSpec as P

HEAD_SIZE = 128
SOFTMAX_SCALE = HEAD_SIZE ** (-0.5)
LOG2_E = math.log2(math.e)
KEY_TILE = 256
HEADS_PER_STEP = 4
VMEM_LIMIT = 40 << 20
F32 = jnp.float32
BF16 = jnp.bfloat16

NT = (((1,), (1,)), ((), ()))
NN = (((1,), (0,)), ((), ()))
TN = (((0,), (0,)), ((), ()))


def dot(a, b, dims):
    return lax.dot_general(a, b, dims, preferred_element_type=F32)


def vmem_params():
    return pltpu.CompilerParams(vmem_limit_bytes=VMEM_LIMIT)


def opening_of(lengths_ref, position):
    total = jnp.int32(0)
    opening = jnp.zeros_like(position)
    for n in range(lengths_ref.shape[1]):
        total = total + lengths_ref[0, n]
        opening = jnp.where(total <= position, total, opening)
    return opening


def prepare_body(
    rank_ref,
    core_ref,
    lengths_ref,
    shift_ref,
    o_ref,
    do_ref,
    features_ref,
    delta_ref,
    norm_ref,
    opening_ref,
    bounds_ref,
    parts_ref,
    sem,
):
    count, _, half = parts_ref.shape
    copies = []
    for n in range(count):
        first = pl.multiple_of((2 * n + core_ref[0]) * half, half)
        copies.append(
            pltpu.make_async_copy(features_ref.at[:, pl.ds(first, half)], parts_ref.at[n], sem.at[n])
        )
        copies[n].start()
    heads, rows = delta_ref.shape[0], delta_ref.shape[2]
    start = rank_ref[0] * rows
    bounds_ref[0] = opening_of(lengths_ref, start)
    bounds_ref[1] = opening_of(lengths_ref, start + rows - 1)
    position = start + lax.broadcasted_iota(jnp.int32, opening_ref.shape, 1)
    opening = opening_of(lengths_ref, position)
    opening_ref[...] = opening
    log_visible = jnp.log((position - opening + 1).astype(F32))[0:1, :]
    for h in range(heads):
        lanes = slice(h * HEAD_SIZE, (h + 1) * HEAD_SIZE)
        product = o_ref[:, lanes].astype(F32) * do_ref[:, lanes].astype(F32)
        delta_ref[h] = jnp.sum(product.T, axis=0, keepdims=True)
        norm_ref[h] = (log_visible + shift_ref[h]) * LOG2_E
    for copy in copies:
        copy.wait()


def prepare(rank, core, lengths, head_shift, o, do, features, parts):
    rows, width = o.shape
    heads = width // HEAD_SIZE
    smem = pl.BlockSpec(memory_space=pltpu.SMEM)
    vmem = pl.BlockSpec(memory_space=pltpu.VMEM)
    return pl.pallas_call(
        prepare_body,
        in_specs=[smem, smem, smem, smem, vmem, vmem, pl.BlockSpec(memory_space=pltpu.HBM)],
        out_specs=[vmem, vmem, vmem, smem, pl.BlockSpec(memory_space=pltpu.HBM)],
        out_shape=[
            jax.ShapeDtypeStruct((heads, 1, rows), F32),
            jax.ShapeDtypeStruct((heads, 1, rows), F32),
            jax.ShapeDtypeStruct((8, rows), jnp.int32),
            jax.ShapeDtypeStruct((2,), jnp.int32),
            jax.ShapeDtypeStruct((parts, rows, features.shape[1] // parts // 2), BF16),
        ],
        scratch_shapes=[pltpu.SemaphoreType.DMA((parts,))],
        compiler_params=vmem_params(),
        name="prepare",
    )(rank, core, lengths, head_shift, o, do, features)


def attention_body(shifts, first, last, *refs):
    blocks = len(shifts)
    rank_ref, bounds_ref, q_ref, do_ref, delta_ref, norm_ref, opening_ref = refs[:7]
    rest = list(refs[7:])
    kv_refs = [rest.pop(0) for _ in range(blocks)]
    dq_in_ref = None if first else rest.pop(0)
    dq_ref = rest.pop(0)
    dkv_refs = [rest.pop(0) for _ in range(blocks)]
    acc_ref, key_t_ref, held_ref, dq_acc_ref = rest
    step = pl.program_id(0)
    rows = q_ref.shape[0]
    start = rank_ref[0] * rows
    first_opening, last_opening = bounds_ref[0], bounds_ref[1]

    @pl.when(step == 0)
    def _():
        acc_ref[...] = jnp.zeros_like(acc_ref)
        for b in range(blocks):
            held_ref[b] = kv_refs[b][...]
            key_t_ref[b] = kv_refs[b][:, :HEAD_SIZE].T

    dq_acc_ref[...] = jnp.zeros_like(dq_acc_ref) if first else dq_in_ref[...]

    def tile(b, key_start, heads, k0, q0, own, masked):
        k = held_ref[b, k0 : k0 + KEY_TILE, :HEAD_SIZE]
        v = held_ref[b, k0 : k0 + KEY_TILE, HEAD_SIZE:]
        if masked:
            shape = (KEY_TILE, rows - q0)
            key = (key_start + k0) + lax.broadcasted_iota(jnp.int32, shape, 0)
            allowed = key >= opening_ref[0:1, q0:]
            if own:
                query = (start + q0) + lax.broadcasted_iota(jnp.int32, shape, 1)
                allowed = allowed & (key <= query)
        for j in heads:
            lanes = pl.ds(j * HEAD_SIZE if isinstance(j, int) else pl.multiple_of(j * HEAD_SIZE, HEAD_SIZE), HEAD_SIZE)
            q = q_ref[q0:, lanes]
            do = do_ref[q0:, lanes]
            scores = dot(k, q, NT)
            probs = jnp.exp2(scores * (SOFTMAX_SCALE * LOG2_E) - norm_ref[j, :, q0:])
            if masked:
                probs = jnp.where(allowed, probs, 0.0)
            prob_grad = dot(v, do, NT)
            score_grad = (probs * (prob_grad - delta_ref[j, :, q0:])).astype(BF16)
            acc_ref[b, k0 : k0 + KEY_TILE, HEAD_SIZE:] += dot(probs.astype(BF16), do, NN)
            acc_ref[b, k0 : k0 + KEY_TILE, :HEAD_SIZE] += dot(score_grad, q, NN)
            dq_acc_ref[j, :, q0:] += dot(key_t_ref[b, :, k0 : k0 + KEY_TILE], score_grad, NN)

    def whole_block(b, key_start):
        for k0 in range(0, rows, KEY_TILE):
            tile(b, key_start, range(HEADS_PER_STEP), k0, 0, False, False)

    def masked_block(b, key_start, own):
        def pair(n, _):
            for k0 in range(0, rows, KEY_TILE):
                tile(b, key_start, (2 * n, 2 * n + 1), k0, k0 if own else 0, own, True)
            return 0

        lax.fori_loop(0, HEADS_PER_STEP // 2, pair, 0)

    def block(b, shift):
        key_start = start - shift * rows
        reached = (key_start >= 0) & (first_opening < key_start + rows)
        whole = last_opening <= key_start

        @pl.when(reached & whole)
        def _():
            whole_block(b, key_start)

        @pl.when(reached & jnp.logical_not(whole))
        def _():
            masked_block(b, key_start, False)

    if shifts == (0,):
        masked_block(0, start, True)
    elif blocks == 1:
        block(0, shifts[0])
    else:

        def each(b, _):
            block(b, jnp.where(b == 0, shifts[0], shifts[1]))
            return 0

        lax.fori_loop(0, blocks, each, 0)

    if last:
        for j in range(HEADS_PER_STEP):
            total = dq_acc_ref[j] * SOFTMAX_SCALE
            dq_ref[:, j * HEAD_SIZE : (j + 1) * HEAD_SIZE] = total.T.astype(BF16)
    else:
        dq_ref[...] = dq_acc_ref[...]

    @pl.when(step == pl.num_programs(0) - 1)
    def _():
        for b in range(blocks):
            dkv_refs[b][:, :HEAD_SIZE] = (acc_ref[b, :, :HEAD_SIZE] * SOFTMAX_SCALE).astype(dkv_refs[b].dtype)
            dkv_refs[b][:, HEAD_SIZE:] = acc_ref[b, :, HEAD_SIZE:].astype(dkv_refs[b].dtype)


def attention_step(shifts, first, last, rank, bounds, q, do, delta, norm, opening, kvs, dq):
    rows, width = q.shape
    heads = width // HEAD_SIZE
    blocks = len(shifts)
    smem = pl.BlockSpec(memory_space=pltpu.SMEM)
    head_block = pl.BlockSpec((rows, HEADS_PER_STEP * HEAD_SIZE), lambda h: (0, h))
    row_block = pl.BlockSpec((HEADS_PER_STEP, 1, rows), lambda h: (h, 0, 0))
    dq_block = pl.BlockSpec((HEADS_PER_STEP, HEAD_SIZE, rows), lambda h: (h, 0, 0))
    kv_block = pl.BlockSpec((rows, 2 * HEAD_SIZE), lambda h: (0, 0))
    opening_block = pl.BlockSpec(opening.shape, lambda h: (0, 0))
    in_specs = [smem, smem, head_block, head_block, row_block, row_block, opening_block]
    in_specs += [kv_block] * blocks + ([] if first else [dq_block])
    if last:
        out_specs = [head_block]
        out_shape = [jax.ShapeDtypeStruct((rows, width), BF16)]
    else:
        out_specs = [dq_block]
        out_shape = [jax.ShapeDtypeStruct((heads, HEAD_SIZE, rows), F32)]
    for s in shifts:
        out_specs.append(kv_block)
        out_shape.append(jax.ShapeDtypeStruct((rows, 2 * HEAD_SIZE), F32 if s == 0 else BF16))
    pairs = heads * rows * rows * blocks
    return pl.pallas_call(
        functools.partial(attention_body, shifts, first, last),
        grid=(heads // HEADS_PER_STEP,),
        in_specs=in_specs,
        out_specs=out_specs,
        out_shape=out_shape,
        scratch_shapes=[
            pltpu.VMEM((blocks, rows, 2 * HEAD_SIZE), F32),
            pltpu.VMEM((blocks, HEAD_SIZE, rows), BF16),
            pltpu.VMEM((blocks, rows, 2 * HEAD_SIZE), BF16),
            pltpu.VMEM((HEADS_PER_STEP, HEAD_SIZE, rows), F32),
        ],
        cost_estimate=pl.CostEstimate(flops=pairs, bytes_accessed=1 << 20, transcendentals=0),
        compiler_params=vmem_params(),
        name="attention_" + "_".join(str(s) for s in shifts),
    )(rank, bounds, q, do, delta, norm, opening, *kvs, *([] if first else [dq]))


def early_sum_body(*refs):
    total = refs[0][...]
    for part in refs[1:-1]:
        total = total + part[...].astype(F32)
    refs[-1][...] = total


def early_sum(own, parts):
    return pl.pallas_call(
        early_sum_body,
        out_shape=jax.ShapeDtypeStruct(own.shape, F32),
        compiler_params=vmem_params(),
        name="early_sum",
    )(own, *parts)


def share_body(early_ref, part_ref, out_ref):
    total = (early_ref[...] + part_ref[...].astype(F32)).astype(BF16)
    for n in range(out_ref.shape[0]):
        out_ref[n] = total


def share_copies(early, part, copies):
    return pl.pallas_call(
        share_body,
        out_shape=jax.ShapeDtypeStruct((copies,) + early.shape, BF16),
        compiler_params=vmem_params(),
        name="share_copies",
    )(early, part)


def product_body(core_ref, own_ref, other_ref, grad_ref, out_ref, acc_ref):
    step = pl.program_id(0)

    @pl.when(step == 0)
    def _():
        acc_ref[...] = jnp.zeros_like(acc_ref)

    grad = grad_ref[...].reshape(-1, grad_ref.shape[2])
    acc_ref[0] += dot(grad, own_ref[...].reshape(-1, own_ref.shape[2]), TN)
    acc_ref[1] += dot(grad, other_ref[...].reshape(-1, other_ref.shape[2]), TN)

    @pl.when(step == pl.num_programs(0) - 1)
    def _():
        low = acc_ref[core_ref[0]].astype(BF16)
        high = acc_ref[1 - core_ref[0]].astype(BF16)
        width = out_ref.shape[2]
        per_half = out_ref.shape[0] // 2
        for c in range(per_half):
            out_ref[c] = low[:, c * width : (c + 1) * width]
            out_ref[per_half + c] = high[:, c * width : (c + 1) * width]


def weight_product(core, own_half, other_half, grads, blocks):
    parts, rows, half = own_half.shape
    cols = grads.shape[2]
    width = 2 * half // blocks
    per_step = 2
    half_block = pl.BlockSpec((per_step, rows, half), lambda d: (d, 0, 0))
    return pl.pallas_call(
        product_body,
        grid=(parts // per_step,),
        in_specs=[
            pl.BlockSpec(memory_space=pltpu.SMEM),
            half_block,
            half_block,
            pl.BlockSpec((per_step, rows, cols), lambda d: (d, 0, 0)),
        ],
        out_specs=pl.BlockSpec((blocks, cols, width), lambda d: (0, 0, 0)),
        out_shape=jax.ShapeDtypeStruct((blocks, cols, width), BF16),
        scratch_shapes=[pltpu.VMEM((2, cols, half), F32)],
        compiler_params=vmem_params(),
        name="weight_product",
    )(core, own_half, other_half, grads)


def codes_body(parts_ref, dither_ref, out_ref):
    total = parts_ref[0].astype(F32)
    for n in range(1, parts_ref.shape[0]):
        total = total + parts_ref[n].astype(F32)
    for k in range(2):
        block = total[k * HEAD_SIZE : (k + 1) * HEAD_SIZE]
        largest = jnp.max(jnp.abs(block))
        scaled = 8.0 * block.T / (largest + 1e-06)
        out_ref[k] = scaled + (dither_ref[k].astype(F32) + 0.5) / 256.0


def weight_codes_of(parts, dither):
    return pl.pallas_call(
        codes_body,
        out_shape=jax.ShapeDtypeStruct(dither.shape, F32),
        compiler_params=vmem_params(),
        name="weight_codes",
    )(parts, dither)


def per_device(
    layer_input,
    queries,
    rotated_key_states,
    values,
    attention_out,
    output_grad,
    normalizer_shift,
    document_lengths,
    dither,
):
    context_size = lax.axis_size("context")
    dp_size = lax.axis_size("dp")
    rank = lax.axis_index("context").astype(jnp.int32).reshape(1)

    def send(x, by, sources=range(context_size)):
        return lax.ppermute(x, "context", [(i, (i + by) % context_size) for i in sources])

    def give_back(x, by):
        return send(x, -by, range(by, context_size))

    own_kv = jnp.concatenate([rotated_key_states[0], values[0]], axis=1)
    kv = {1: send(own_kv, 1), 6: send(own_kv, -2)}

    q, do = queries[0], output_grad[0]
    core = (lax.axis_index("tensor") % 2).astype(jnp.int32).reshape(1)
    delta, norm, opening, bounds, features = prepare(
        rank, core, document_lengths, normalizer_shift, attention_out[0], do, layer_input[0], dp_size
    )
    kv[1], kv[6], delta, features = lax.optimization_barrier((kv[1], kv[6], delta, features))
    own_half = lax.all_to_all(features, "dp", 0, 0)
    step = functools.partial(
        attention_step, rank=rank, bounds=bounds, q=q, do=do, delta=delta, norm=norm, opening=opening
    )
    back = []
    kv[2] = send(kv[1], 1)
    dq, term = step((1,), True, False, kvs=[kv[1]], dq=None)
    back.append(give_back(term, 1))
    kv[2], kv[6], dq = lax.optimization_barrier((kv[2], kv[6], dq))
    kv[3] = send(kv[2], 1)
    kv[5] = send(kv[6], -1)

    def work(shifts, dq):
        dq, *terms = step(shifts, False, False, kvs=[kv[s] for s in shifts], dq=dq)
        return dq, [give_back(term, s) for s, term in zip(shifts, terms, strict=True)]

    dq, terms = work((2, 6), dq)
    back += terms
    kv[3], kv[5], dq = lax.optimization_barrier((kv[3], kv[5], dq))
    kv[4] = send(kv[3], 1, range(3, context_size - 1))
    dq, middle = work((3, 5), dq)
    back += middle
    dq, (last,) = work((4,), dq)
    dq, own = step((0,), False, True, kvs=[own_kv], dq=dq)

    grads = share_copies(early_sum(own, back), last, dp_size)
    own_half, grads = lax.optimization_barrier((own_half, grads))
    swap = [(t, t ^ 1) for t in range(lax.axis_size("tensor"))]
    other_half = lax.ppermute(own_half, "tensor", swap)
    grads = lax.all_to_all(grads, "dp", 0, 0)
    product = weight_product(core, own_half, other_half, grads, context_size)
    parts = lax.all_to_all(product, "context", 0, 0)
    weight_codes = weight_codes_of(parts, dither)
    return (dq[None], weight_codes)


def solution(mesh):
    placed = (
        P("dp", "context", None),
        P("dp", "context", "tensor"),
        P("dp", "context", "tensor"),
        P("dp", "context", "tensor"),
        P("dp", "context", "tensor"),
        P("dp", "context", "tensor"),
        P("tensor"),
        P("dp", None),
        P(None, ("dp", "context"), "tensor"),
    )
    return jax.shard_map(
        per_device,
        mesh=mesh,
        in_specs=placed,
        out_specs=(P("dp", "context", "tensor"), P(None, ("dp", "context"), "tensor")),
        check_vma=False,
    )
```

```python
import functools
import math

import jax
import jax.numpy as jnp
from jax import lax
from jax.experimental import pallas as pl
from jax.experimental.pallas import tpu as pltpu
from jax.sharding import PartitionSpec as P

HEAD_SIZE = 128
SOFTMAX_SCALE = HEAD_SIZE ** (-0.5)
LOG2_E = math.log2(math.e)
KEY_TILE = 256
HEADS_PER_STEP = 4
VMEM_LIMIT = 40 << 20
F32 = jnp.float32
BF16 = jnp.bfloat16

NT = (((1,), (1,)), ((), ()))
NN = (((1,), (0,)), ((), ()))
TN = (((0,), (0,)), ((), ()))


def dot(a, b, dims):
    return lax.dot_general(a, b, dims, preferred_element_type=F32)


def vmem_params():
    return pltpu.CompilerParams(vmem_limit_bytes=VMEM_LIMIT)


def opening_of(lengths_ref, position):
    total = jnp.int32(0)
    opening = jnp.zeros_like(position)
    for n in range(lengths_ref.shape[1]):
        total = total + lengths_ref[0, n]
        opening = jnp.where(total <= position, total, opening)
    return opening


def prepare_body(
    rank_ref,
    core_ref,
    lengths_ref,
    shift_ref,
    o_ref,
    do_ref,
    features_ref,
    delta_ref,
    norm_ref,
    opening_ref,
    bounds_ref,
    parts_ref,
    sem,
):
    count, _, half = parts_ref.shape
    copies = []
    for n in range(count):
        first = pl.multiple_of((2 * n + core_ref[0]) * half, half)
        copies.append(
            pltpu.make_async_copy(features_ref.at[:, pl.ds(first, half)], parts_ref.at[n], sem.at[n])
        )
        copies[n].start()
    heads, rows = delta_ref.shape[0], delta_ref.shape[2]
    start = rank_ref[0] * rows
    bounds_ref[0] = opening_of(lengths_ref, start)
    bounds_ref[1] = opening_of(lengths_ref, start + rows - 1)
    position = start + lax.broadcasted_iota(jnp.int32, opening_ref.shape, 1)
    opening = opening_of(lengths_ref, position)
    opening_ref[...] = opening
    log_visible = jnp.log((position - opening + 1).astype(F32))[0:1, :]
    for h in range(heads):
        lanes = slice(h * HEAD_SIZE, (h + 1) * HEAD_SIZE)
        product = o_ref[:, lanes].astype(F32) * do_ref[:, lanes].astype(F32)
        delta_ref[h] = jnp.sum(product.T, axis=0, keepdims=True)
        norm_ref[h] = (log_visible + shift_ref[h]) * LOG2_E
    for copy in copies:
        copy.wait()


def prepare(rank, core, lengths, head_shift, o, do, features, parts):
    rows, width = o.shape
    heads = width // HEAD_SIZE
    smem = pl.BlockSpec(memory_space=pltpu.SMEM)
    vmem = pl.BlockSpec(memory_space=pltpu.VMEM)
    return pl.pallas_call(
        prepare_body,
        in_specs=[smem, smem, smem, smem, vmem, vmem, pl.BlockSpec(memory_space=pltpu.HBM)],
        out_specs=[vmem, vmem, vmem, smem, pl.BlockSpec(memory_space=pltpu.HBM)],
        out_shape=[
            jax.ShapeDtypeStruct((heads, 1, rows), F32),
            jax.ShapeDtypeStruct((heads, 1, rows), F32),
            jax.ShapeDtypeStruct((8, rows), jnp.int32),
            jax.ShapeDtypeStruct((2,), jnp.int32),
            jax.ShapeDtypeStruct((parts, rows, features.shape[1] // parts // 2), BF16),
        ],
        scratch_shapes=[pltpu.SemaphoreType.DMA((parts,))],
        compiler_params=vmem_params(),
        name="prepare",
    )(rank, core, lengths, head_shift, o, do, features)


def attention_body(shifts, first, last, *refs):
    blocks = len(shifts)
    rank_ref, bounds_ref, q_ref, do_ref, delta_ref, norm_ref, opening_ref = refs[:7]
    rest = list(refs[7:])
    kv_refs = [rest.pop(0) for _ in range(blocks)]
    dq_in_ref = None if first else rest.pop(0)
    dq_ref = rest.pop(0)
    dkv_refs = [rest.pop(0) for _ in range(blocks)]
    acc_ref, key_t_ref, held_ref, dq_acc_ref = rest
    step = pl.program_id(0)
    rows = q_ref.shape[0]
    start = rank_ref[0] * rows
    first_opening, last_opening = bounds_ref[0], bounds_ref[1]

    @pl.when(step == 0)
    def _():
        acc_ref[...] = jnp.zeros_like(acc_ref)
        for b in range(blocks):
            held_ref[b] = kv_refs[b][...]
            key_t_ref[b] = kv_refs[b][:, :HEAD_SIZE].T

    dq_acc_ref[...] = jnp.zeros_like(dq_acc_ref) if first else dq_in_ref[...]

    def tile(b, key_start, heads, k0, q0, own, masked):
        k = held_ref[b, k0 : k0 + KEY_TILE, :HEAD_SIZE]
        v = held_ref[b, k0 : k0 + KEY_TILE, HEAD_SIZE:]
        if masked:
            shape = (KEY_TILE, rows - q0)
            key = (key_start + k0) + lax.broadcasted_iota(jnp.int32, shape, 0)
            allowed = key >= opening_ref[0:1, q0:]
            if own:
                query = (start + q0) + lax.broadcasted_iota(jnp.int32, shape, 1)
                allowed = allowed & (key <= query)
        for j in heads:
            lanes = pl.ds(j * HEAD_SIZE if isinstance(j, int) else pl.multiple_of(j * HEAD_SIZE, HEAD_SIZE), HEAD_SIZE)
            q = q_ref[q0:, lanes]
            do = do_ref[q0:, lanes]
            scores = dot(k, q, NT)
            probs = jnp.exp2(scores * (SOFTMAX_SCALE * LOG2_E) - norm_ref[j, :, q0:])
            if masked:
                probs = jnp.where(allowed, probs, 0.0)
            prob_grad = dot(v, do, NT)
            score_grad = (probs * (prob_grad - delta_ref[j, :, q0:])).astype(BF16)
            acc_ref[b, k0 : k0 + KEY_TILE, HEAD_SIZE:] += dot(probs.astype(BF16), do, NN)
            acc_ref[b, k0 : k0 + KEY_TILE, :HEAD_SIZE] += dot(score_grad, q, NN)
            dq_acc_ref[j, :, q0:] += dot(key_t_ref[b, :, k0 : k0 + KEY_TILE], score_grad, NN)

    def whole_block(b, key_start):
        for k0 in range(0, rows, KEY_TILE):
            tile(b, key_start, range(HEADS_PER_STEP), k0, 0, False, False)

    def masked_block(b, key_start, own):
        def pair(n, _):
            for k0 in range(0, rows, KEY_TILE):
                tile(b, key_start, (2 * n, 2 * n + 1), k0, k0 if own else 0, own, True)
            return 0

        lax.fori_loop(0, HEADS_PER_STEP // 2, pair, 0)

    def block(b, shift):
        key_start = start - shift * rows
        reached = (key_start >= 0) & (first_opening < key_start + rows)
        whole = last_opening <= key_start

        @pl.when(reached & whole)
        def _():
            whole_block(b, key_start)

        @pl.when(reached & jnp.logical_not(whole))
        def _():
            masked_block(b, key_start, False)

    if shifts == (0,):
        masked_block(0, start, True)
    elif min(shifts) > 2 or blocks == 1:
        for b in range(blocks):
            block(b, shifts[b])
    else:

        def each(b, _):
            block(b, jnp.where(b == 0, shifts[0], shifts[1]))
            return 0

        lax.fori_loop(0, blocks, each, 0)

    if last:
        for j in range(HEADS_PER_STEP):
            total = dq_acc_ref[j] * SOFTMAX_SCALE
            dq_ref[:, j * HEAD_SIZE : (j + 1) * HEAD_SIZE] = total.T.astype(BF16)
    else:
        dq_ref[...] = dq_acc_ref[...]

    @pl.when(step == pl.num_programs(0) - 1)
    def _():
        for b in range(blocks):
            dkv_refs[b][:, :HEAD_SIZE] = (acc_ref[b, :, :HEAD_SIZE] * SOFTMAX_SCALE).astype(dkv_refs[b].dtype)
            dkv_refs[b][:, HEAD_SIZE:] = acc_ref[b, :, HEAD_SIZE:].astype(dkv_refs[b].dtype)


def attention_step(shifts, first, last, rank, bounds, q, do, delta, norm, opening, kvs, dq):
    rows, width = q.shape
    heads = width // HEAD_SIZE
    blocks = len(shifts)
    smem = pl.BlockSpec(memory_space=pltpu.SMEM)
    head_block = pl.BlockSpec((rows, HEADS_PER_STEP * HEAD_SIZE), lambda h: (0, h))
    row_block = pl.BlockSpec((HEADS_PER_STEP, 1, rows), lambda h: (h, 0, 0))
    dq_block = pl.BlockSpec((HEADS_PER_STEP, HEAD_SIZE, rows), lambda h: (h, 0, 0))
    kv_block = pl.BlockSpec((rows, 2 * HEAD_SIZE), lambda h: (0, 0))
    opening_block = pl.BlockSpec(opening.shape, lambda h: (0, 0))
    in_specs = [smem, smem, head_block, head_block, row_block, row_block, opening_block]
    in_specs += [kv_block] * blocks + ([] if first else [dq_block])
    if last:
        out_specs = [head_block]
        out_shape = [jax.ShapeDtypeStruct((rows, width), BF16)]
    else:
        out_specs = [dq_block]
        out_shape = [jax.ShapeDtypeStruct((heads, HEAD_SIZE, rows), F32)]
    for s in shifts:
        out_specs.append(kv_block)
        out_shape.append(jax.ShapeDtypeStruct((rows, 2 * HEAD_SIZE), F32 if s == 0 else BF16))
    pairs = heads * rows * rows * blocks
    return pl.pallas_call(
        functools.partial(attention_body, shifts, first, last),
        grid=(heads // HEADS_PER_STEP,),
        in_specs=in_specs,
        out_specs=out_specs,
        out_shape=out_shape,
        scratch_shapes=[
            pltpu.VMEM((blocks, rows, 2 * HEAD_SIZE), F32),
            pltpu.VMEM((blocks, HEAD_SIZE, rows), BF16),
            pltpu.VMEM((blocks, rows, 2 * HEAD_SIZE), BF16),
            pltpu.VMEM((HEADS_PER_STEP, HEAD_SIZE, rows), F32),
        ],
        cost_estimate=pl.CostEstimate(flops=pairs, bytes_accessed=1 << 20, transcendentals=0),
        compiler_params=vmem_params(),
        name="attention_" + "_".join(str(s) for s in shifts),
    )(rank, bounds, q, do, delta, norm, opening, *kvs, *([] if first else [dq]))


def early_sum_body(*refs):
    total = refs[0][...]
    for part in refs[1:-1]:
        total = total + part[...].astype(F32)
    refs[-1][...] = total


def early_sum(own, parts):
    return pl.pallas_call(
        early_sum_body,
        out_shape=jax.ShapeDtypeStruct(own.shape, F32),
        compiler_params=vmem_params(),
        name="early_sum",
    )(own, *parts)


def share_body(early_ref, part_ref, out_ref):
    total = (early_ref[...] + part_ref[...].astype(F32)).astype(BF16)
    for n in range(out_ref.shape[0]):
        out_ref[n] = total


def share_copies(early, part, copies):
    return pl.pallas_call(
        share_body,
        out_shape=jax.ShapeDtypeStruct((copies,) + early.shape, BF16),
        compiler_params=vmem_params(),
        name="share_copies",
    )(early, part)


def product_body(core_ref, own_ref, other_ref, grad_ref, out_ref, acc_ref):
    step = pl.program_id(0)

    @pl.when(step == 0)
    def _():
        acc_ref[...] = jnp.zeros_like(acc_ref)

    grad = grad_ref[...].reshape(-1, grad_ref.shape[2])
    acc_ref[0] += dot(grad, own_ref[...].reshape(-1, own_ref.shape[2]), TN)
    acc_ref[1] += dot(grad, other_ref[...].reshape(-1, other_ref.shape[2]), TN)

    @pl.when(step == pl.num_programs(0) - 1)
    def _():
        low = acc_ref[core_ref[0]].astype(BF16)
        high = acc_ref[1 - core_ref[0]].astype(BF16)
        width = out_ref.shape[2]
        per_half = out_ref.shape[0] // 2
        for c in range(per_half):
            out_ref[c] = low[:, c * width : (c + 1) * width]
            out_ref[per_half + c] = high[:, c * width : (c + 1) * width]


def weight_product(core, own_half, other_half, grads, blocks):
    parts, rows, half = own_half.shape
    cols = grads.shape[2]
    width = 2 * half // blocks
    per_step = 2
    half_block = pl.BlockSpec((per_step, rows, half), lambda d: (d, 0, 0))
    return pl.pallas_call(
        product_body,
        grid=(parts // per_step,),
        in_specs=[
            pl.BlockSpec(memory_space=pltpu.SMEM),
            half_block,
            half_block,
            pl.BlockSpec((per_step, rows, cols), lambda d: (d, 0, 0)),
        ],
        out_specs=pl.BlockSpec((blocks, cols, width), lambda d: (0, 0, 0)),
        out_shape=jax.ShapeDtypeStruct((blocks, cols, width), BF16),
        scratch_shapes=[pltpu.VMEM((2, cols, half), F32)],
        compiler_params=vmem_params(),
        name="weight_product",
    )(core, own_half, other_half, grads)


def codes_body(parts_ref, dither_ref, out_ref):
    total = parts_ref[0].astype(F32)
    for n in range(1, parts_ref.shape[0]):
        total = total + parts_ref[n].astype(F32)
    for k in range(2):
        block = total[k * HEAD_SIZE : (k + 1) * HEAD_SIZE]
        largest = jnp.max(jnp.abs(block))
        scaled = 8.0 * block.T / (largest + 1e-06)
        out_ref[k] = scaled + (dither_ref[k].astype(F32) + 0.5) / 256.0


def weight_codes_of(parts, dither):
    return pl.pallas_call(
        codes_body,
        out_shape=jax.ShapeDtypeStruct(dither.shape, F32),
        compiler_params=vmem_params(),
        name="weight_codes",
    )(parts, dither)


def per_device(
    layer_input,
    queries,
    rotated_key_states,
    values,
    attention_out,
    output_grad,
    normalizer_shift,
    document_lengths,
    dither,
):
    context_size = lax.axis_size("context")
    dp_size = lax.axis_size("dp")
    rank = lax.axis_index("context").astype(jnp.int32).reshape(1)

    def send(x, by, sources=range(context_size)):
        return lax.ppermute(x, "context", [(i, (i + by) % context_size) for i in sources])

    def give_back(x, by):
        return send(x, -by, range(by, context_size))

    own_kv = jnp.concatenate([rotated_key_states[0], values[0]], axis=1)
    kv = {1: send(own_kv, 1), 6: send(own_kv, -2)}

    q, do = queries[0], output_grad[0]
    core = (lax.axis_index("tensor") % 2).astype(jnp.int32).reshape(1)
    delta, norm, opening, bounds, features = prepare(
        rank, core, document_lengths, normalizer_shift, attention_out[0], do, layer_input[0], dp_size
    )
    kv[1], kv[6], delta, features = lax.optimization_barrier((kv[1], kv[6], delta, features))
    own_half = lax.all_to_all(features, "dp", 0, 0)
    step = functools.partial(
        attention_step, rank=rank, bounds=bounds, q=q, do=do, delta=delta, norm=norm, opening=opening
    )
    back = []
    kv[2] = send(kv[1], 1)
    dq, term = step((1,), True, False, kvs=[kv[1]], dq=None)
    back.append(give_back(term, 1))
    kv[2], kv[6], dq = lax.optimization_barrier((kv[2], kv[6], dq))
    kv[3] = send(kv[2], 1)
    kv[5] = send(kv[6], -1)

    def work(shifts, dq):
        dq, *terms = step(shifts, False, False, kvs=[kv[s] for s in shifts], dq=dq)
        return dq, [give_back(term, s) for s, term in zip(shifts, terms, strict=True)]

    dq, terms = work((2, 6), dq)
    back += terms
    kv[3], kv[5], dq = lax.optimization_barrier((kv[3], kv[5], dq))
    kv[4] = send(kv[3], 1, range(3, context_size - 1))
    dq, middle = work((3, 5), dq)
    back += middle
    dq, (last,) = work((4,), dq)
    dq, own = step((0,), False, True, kvs=[own_kv], dq=dq)

    grads = share_copies(early_sum(own, back), last, dp_size)
    own_half, grads = lax.optimization_barrier((own_half, grads))
    swap = [(t, t ^ 1) for t in range(lax.axis_size("tensor"))]
    other_half = lax.ppermute(own_half, "tensor", swap)
    grads = lax.all_to_all(grads, "dp", 0, 0)
    product = weight_product(core, own_half, other_half, grads, context_size)
    parts = lax.all_to_all(product, "context", 0, 0)
    weight_codes = weight_codes_of(parts, dither)
    return (dq[None], weight_codes)


def solution(mesh):
    placed = (
        P("dp", "context", None),
        P("dp", "context", "tensor"),
        P("dp", "context", "tensor"),
        P("dp", "context", "tensor"),
        P("dp", "context", "tensor"),
        P("dp", "context", "tensor"),
        P("tensor"),
        P("dp", None),
        P(None, ("dp", "context"), "tensor"),
    )
    return jax.shard_map(
        per_device,
        mesh=mesh,
        in_specs=placed,
        out_specs=(P("dp", "context", "tensor"), P(None, ("dp", "context"), "tensor")),
        check_vma=False,
    )
```
